256 devices in a mesh: latent: 32 (over z, x), replica: 8 (over y, core).
Axes of the slice: x: 4, y: 4, z: 8, core: 2. Of those that a mesh axis runs over, the one named last changes fastest.
Arguments:
- tokens: bfloat16 [131072, 2048], P(('replica', 'latent')), may hold values from -6 to 6
- block_ids: int32 [131072, 2], P(('replica', 'latent')), may hold values from 0 to 255, as said below
- enc_bias: float32 [16384], P('latent'), may hold values from -1 to 0.5
- enc_master: float32 [2048, 16384], P('replica', 'latent'), may hold values from -0.125 to 0.125
- dec_master: float32 [16384, 2048], P('latent', 'replica'), may hold values from -0.5 to 0.5
- enc_first: float32 [2048, 16384], P('replica', 'latent'), may hold values from -256 to 256
- enc_second: float32 [2048, 16384], P('replica', 'latent'), may hold values from 1000 to 20000
- dec_first: float32 [16384, 2048], P('latent', 'replica'), may hold values from -32 to 32
- dec_second: float32 [16384, 2048], P('latent', 'replica'), may hold values from 20 to 400
Outputs:
- enc_master_new: float32 [2048, 16384], P('replica', 'latent')
- dec_master_new: float32 [16384, 2048], P('latent', 'replica')
- enc_first_new: float32 [2048, 16384], P('replica', 'latent')
- enc_second_new: float32 [2048, 16384], P('replica', 'latent')
- decoder_first_moment_next: float32 [16384, 2048], P('latent', 'replica')
- dec_second_new: float32 [16384, 2048], P('latent', 'replica')
The draws below stay inside these ranges and needn't reach their ends.
Inputs may be any that keep to these rules, and one draw needn't show every extreme that they name: `block_ids`: each row names 2 different blocks. Among the 512 rows of one device (aligned blocks of rows), no block is named by more than 5 rows, and in every such group of rows some block is named by exactly 5 rows.
All inputs are finite; a program needn't handle non-finite values.
Results may differ from the reference program's by a relative error of at most 0.0041.
Values may be sent and summed in bfloat16 or wider, within the bound.
A program may use at most 128 MiB of HBM per device.

```python
import math
import jax
import jax.numpy as jnp
from jax import lax

D = 2048
BLOCK = 64
ACT = 2
TOK_DEV = 512
NBLK = 256
CAP = 5
LATENTS = 16384
TOKENS = 131072
N_LATENT = 32
N_REPLICA = 8


def draw_block_ids(key, part):
    key = jax.random.fold_in(key, 11)
    span_count = TOKENS // TOK_DEV
    key_common, key_rest = jax.random.split(key)
    common_block = jax.random.randint(key_common, (), 0, NBLK).astype(jnp.int32)
    span_keys = jax.random.split(key_rest, span_count)

    def one_span(sub):
        key_keep, key_label, key_order, key_roll = jax.random.split(sub, 4)
        spare = jax.random.permutation(key_keep, NBLK * CAP - CAP).astype(jnp.int32) + CAP
        kept = jnp.concatenate([jnp.arange(CAP, dtype=jnp.int32), spare[:TOK_DEV * ACT - CAP]])
        kept = jnp.sort(kept)
        labels = (kept // CAP).astype(jnp.int32)
        relabel = jax.random.permutation(key_label, NBLK).astype(jnp.int32)
        relabel = jnp.where(relabel == common_block, relabel[0], relabel)
        relabel = relabel.at[0].set(common_block)
        labels = relabel[labels]
        table = labels.reshape(ACT, TOK_DEV).T
        order = jax.random.permutation(key_order, TOK_DEV).astype(jnp.int32)
        table = table[order]
        rolls = jax.random.randint(key_roll, (TOK_DEV,), 0, ACT).astype(jnp.int32)
        columns = (jnp.arange(ACT, dtype=jnp.int32)[None, :] + rolls[:, None]) % ACT
        table = jnp.take_along_axis(table, columns, axis=1)
        return table.astype(jnp.int32)
    return jax.vmap(one_span)(span_keys).reshape(TOKENS, ACT).astype(jnp.int32)


def block_levels(own_key, extent, shards, smallest, largest):
    loudness, own = 1.0, jax.random.fold_in(own_key, 6)
    for position, shards_of in shards:
        draws = jnp.exp(jax.random.uniform(jax.random.fold_in(own, position), (shards_of,), jnp.float32, smallest / len(shards), largest / len(shards)))
        loudness = loudness * jnp.repeat(draws, extent[position] // shards_of).reshape([-1 if axis == position else 1 for axis in range(len(extent))])
    return loudness


def normal_values(rng, extent, width, most, pieces=(), kind=jnp.bfloat16):
    entries = jax.random.normal(rng, extent, jnp.float32) * width
    if len(pieces) > 0:
        entries = block_levels(rng, extent, pieces, -0.22, 0.18) * entries
    return jnp.clip(entries, min=-most, max=most).astype(kind)


def setup_inputs(seed: int = 0) -> dict:
    splits = jax.random.split(jax.random.key(seed), 10)
    return {
        "tokens": normal_values(splits[0], (TOKENS, D), 1.0, 6.0, ((0, 256),)),
        "block_ids": draw_block_ids(jax.random.fold_in(splits[9], 71), 0),
        "enc_bias": jnp.clip(-1.0 + 1.5 * jax.random.uniform(splits[2], (LATENTS,), jnp.float32) ** block_levels(splits[2], (LATENTS,), ((0, 32),), -0.2, 0.2), -1.0, 0.5),
        "enc_master": normal_values(splits[3], (D, LATENTS), D ** -0.5, 0.125, ((0, 8), (1, 32)), jnp.float32),
        "dec_master": normal_values(splits[4], (LATENTS, D), (ACT * BLOCK) ** -0.5, 0.5, ((0, 32), (1, 8)), jnp.float32),
        "enc_first": normal_values(splits[5], (D, LATENTS), 40.0, 256.0, ((0, 8), (1, 32)), jnp.float32),
        "enc_second": jnp.clip(jnp.exp(math.log(20000.0) - 2.9957323 * jax.random.uniform(splits[6], (D, LATENTS), jnp.float32) ** block_levels(splits[6], (D, LATENTS), ((0, 8), (1, 32)), -0.2, 0.2)), 1000.0, 20000.0),
        "dec_first": normal_values(splits[7], (LATENTS, D), 6.0, 32.0, ((0, 32), (1, 8)), jnp.float32),
        "dec_second": jnp.clip(jnp.exp(math.log(400.0) - 2.9957323 * jax.random.uniform(splits[8], (LATENTS, D), jnp.float32) ** block_levels(splits[8], (LATENTS, D), ((0, 32), (1, 8)), -0.2, 0.2)), 20.0, 400.0),
    }


learn_rate = 0.001
adam_eps = 1e-08
first_fix = 1.0 - 0.9 ** 10
second_fix = 1.0 - 0.95 ** 10

def select_rows(block_list, block_nums, capacity):
    count_rows = block_list.shape[0]
    chosen = jnp.any(block_list[None, :, :] == block_nums[:, None, None], axis=-1)
    places = jnp.cumsum(chosen.astype(jnp.int32), axis=1) - 1
    slot_nums = jnp.arange(capacity, dtype=jnp.int32)
    select = chosen[:, None, :] & (places[:, None, :] == slot_nums[None, :, None])
    row_nums = jnp.arange(count_rows, dtype=jnp.int32)
    slot_rows = lax.optimization_barrier(jnp.sum(jnp.where(select, row_nums[None, None, :], 0), axis=-1)).astype(jnp.int32)
    filled = jnp.any(select, axis=-1)
    return (slot_rows, filled)

def activate(preact, filled):
    values_out, slopes = jax.jvp(lambda inner: jax.nn.gelu(inner, approximate=True), (preact,), (jnp.ones_like(preact),))
    latent_codes_active = jnp.where(filled[..., None], values_out, 0.0).astype(jnp.bfloat16)
    return (latent_codes_active, jnp.where(filled[..., None], slopes, 0.0))

def adam(master_weights_full, gradient, first, second):
    first_new = 0.9 * first + 0.1 * gradient
    second_new = 0.95 * second + 0.05 * gradient * gradient
    update = first_new / first_fix / (jnp.sqrt(second_new / second_fix) + adam_eps)
    return (master_weights_full - learn_rate * update, first_new, second_new)

def reference(tokens, block_ids, enc_bias, enc_master, dec_master, enc_first, enc_second, dec_first, dec_second):
    groups = N_REPLICA * N_LATENT
    enc_weight = enc_master.astype(jnp.bfloat16)
    dec_weight = dec_master.astype(jnp.bfloat16)
    grouped = tokens.reshape(groups, TOK_DEV, D)
    grouped_ids = block_ids.reshape(groups, TOK_DEV, ACT)
    group_nums = jnp.arange(groups, dtype=jnp.int32)[:, None]

    def forward_block(number):
        slot_rows, filled = jax.vmap(lambda block_list: select_rows(block_list, number.reshape(1), CAP))(grouped_ids)
        slot_rows = slot_rows[:, 0, :]
        filled = filled[:, 0, :]
        picked = jnp.take_along_axis(grouped, slot_rows[..., None], axis=1)
        enc_block = lax.dynamic_slice_in_dim(enc_weight, number * BLOCK, BLOCK, 1)
        dec_block = lax.dynamic_slice_in_dim(dec_weight, number * BLOCK, BLOCK, 0)
        bias_block = lax.dynamic_slice_in_dim(enc_bias, number * BLOCK, BLOCK, 0)
        preact = jnp.einsum('gcd,dk->gck', picked.astype(jnp.float32), enc_block.astype(jnp.float32)) + bias_block[None, None, :]
        latent_codes_active, slopes = activate(preact, filled)
        return (slot_rows, picked, dec_block, latent_codes_active, slopes)

    def add_block(rebuilt, number):
        slot_rows, picked, dec_block, latent_codes_active, slopes = forward_block(number)
        contrib = jnp.einsum('gck,kd->gcd', latent_codes_active.astype(jnp.float32), dec_block.astype(jnp.float32))
        contrib = lax.optimization_barrier(contrib.astype(jnp.bfloat16)).astype(jnp.float32)
        return (rebuilt.at[group_nums, slot_rows].add(contrib), None)
    numbers = jnp.arange(NBLK, dtype=jnp.int32)
    rebuilt, unused = lax.scan(add_block, jnp.zeros((groups, TOK_DEV, D), jnp.float32), numbers)
    error_rows = (rebuilt - grouped.astype(jnp.float32)).astype(jnp.bfloat16)

    def grad_block(carry, number):
        slot_rows, picked, dec_block, latent_codes_active, slopes = forward_block(number)
        picked_err = jnp.take_along_axis(error_rows, slot_rows[..., None], axis=1).astype(jnp.float32)
        coded_grad = jnp.einsum('gcd,kd->gck', picked_err, dec_block.astype(jnp.float32))
        pre_grad = (coded_grad * slopes).astype(jnp.bfloat16)
        decoder_portion = jnp.einsum('gck,gcd->kd', latent_codes_active.astype(jnp.float32), picked_err)
        enc_part = jnp.einsum('gcd,gck->dk', picked.astype(jnp.float32), pre_grad.astype(jnp.float32))
        return (carry, (enc_part, decoder_portion))
    unused, (enc_parts, dec_parts) = lax.scan(grad_block, jnp.zeros((), jnp.float32), numbers)
    dec_grad = dec_parts.reshape(LATENTS, D)
    enc_grad = jnp.transpose(enc_parts, (1, 0, 2)).reshape(D, LATENTS)
    enc_master_new, enc_first_new, enc_second_new = adam(enc_master, enc_grad, enc_first, enc_second)
    dec_master_new, decoder_first_moment_next, dec_second_new = adam(dec_master, dec_grad, dec_first, dec_second)
    return (enc_master_new, dec_master_new, enc_first_new, enc_second_new, decoder_first_moment_next, dec_second_new)
```

```python
import jax
import jax.numpy as jnp
from jax import lax
from jax.sharding import Mesh, PartitionSpec as P

BLOCK = 64
CAP = 5

learn_rate = 0.001
adam_eps = 1e-08
first_fix = 1.0 - 0.9**10
second_fix = 1.0 - 0.95**10

PLANE = ("x", "y", "c")
REP = ("y", "c")


def adam(master, gradient, first, second):
    first_new = 0.9 * first + 0.1 * gradient
    second_new = 0.95 * second + 0.05 * gradient * gradient
    update = first_new / first_fix / (jnp.sqrt(second_new / second_fix) + adam_eps)
    return (master - learn_rate * update, first_new, second_new)


def slot_onehot(block_ids, block_nums):
    chosen = jnp.any(block_ids[None, :, :] == block_nums[:, None, None], axis=-1)
    places = jnp.cumsum(chosen.astype(jnp.int32), axis=1) - 1
    slots = jnp.arange(CAP, dtype=jnp.int32)
    return chosen[:, None, :] & (places[:, None, :] == slots[None, :, None])


def dot(a, b, ca, cb, out=jnp.float32):
    return lax.dot_general(a, b, (((ca,), (cb,)), ((), ())), preferred_element_type=out)


def local(
    tokens,
    block_ids,
    enc_bias,
    enc_master,
    dec_master,
    enc_first,
    enc_second,
    dec_first,
    dec_second,
):
    nz, nx = lax.axis_size("z"), lax.axis_size("x")
    nrep = lax.axis_size("y") * lax.axis_size("c")
    plane = nx * nrep
    tok, width = tokens.shape
    lat = enc_master.shape[1]
    part = width // nrep
    rep = lax.axis_index("y") * lax.axis_size("c") + lax.axis_index("c")

    def spread(w):
        w = w.reshape(nrep, BLOCK, part)
        w = lax.all_to_all(w, REP, split_axis=0, concat_axis=2, tiled=True)
        return lax.all_gather(w, "z", axis=0, tiled=True).reshape(nz * BLOCK, width)

    enc_t = spread(enc_master.astype(jnp.bfloat16).T)
    dec = spread(dec_master.astype(jnp.bfloat16))
    own_bias = lax.dynamic_slice(enc_bias, (rep * BLOCK,), (BLOCK,))
    bias = lax.all_gather(own_bias, "z", axis=0, tiled=True)

    nums = jnp.arange(nz * plane, dtype=jnp.int32).reshape(nz, plane).T.reshape(-1)
    onehot = slot_onehot(block_ids, nums).reshape(nz * plane * CAP, tok).astype(jnp.bfloat16)

    def exchange(rows):
        rows = rows.reshape(plane, nz * CAP, width)
        return lax.all_to_all(rows, PLANE, split_axis=0, concat_axis=0, tiled=True).reshape(
            plane * nz * CAP, width
        )

    arrived = exchange(dot(onehot, tokens, 1, 0, jnp.bfloat16))
    count = arrived.shape[0]
    own = (lax.broadcasted_iota(jnp.int32, (count, lat), 0) % (nz * CAP)) // CAP == (
        lax.broadcasted_iota(jnp.int32, (count, lat), 1) // BLOCK
    )
    preact = dot(arrived, enc_t, 1, 1) + bias[None, :]
    values, slopes = jax.jvp(
        lambda inner: jax.nn.gelu(inner, approximate=True), (preact,), (jnp.ones_like(preact),)
    )
    coded = jnp.where(own, values, 0.0).astype(jnp.bfloat16)
    slopes = jnp.where(own, slopes, 0.0)
    contrib = dot(coded, dec, 1, 0).astype(jnp.bfloat16)
    returned = exchange(contrib)
    rebuilt = dot(onehot, returned, 0, 0)
    error_rows = (rebuilt - tokens.astype(jnp.float32)).astype(jnp.bfloat16)
    err_in = exchange(dot(onehot, error_rows, 1, 0, jnp.bfloat16))
    dec_grad = dot(coded, err_in, 0, 0)
    pre_grad = (dot(err_in, dec, 1, 1) * slopes).astype(jnp.bfloat16)
    enc_grad = dot(pre_grad, arrived, 0, 0)

    def collect(g):
        g = g.astype(jnp.bfloat16).reshape(nz, BLOCK, width)
        g = lax.all_to_all(g, "z", split_axis=0, concat_axis=0, tiled=True)
        g = jnp.sum(g.astype(jnp.float32), axis=0)
        g = lax.all_to_all(g, REP, split_axis=1, concat_axis=0, tiled=True)
        return g.reshape(lat, part)

    dec_share = collect(dec_grad)
    enc_share = collect(enc_grad).T
    enc_new, enc_first_new, enc_second_new = adam(enc_master, enc_share, enc_first, enc_second)
    dec_new, dec_first_new, dec_second_new = adam(dec_master, dec_share, dec_first, dec_second)
    return (enc_new, dec_new, enc_first_new, enc_second_new, dec_first_new, dec_second_new)


def solution(mesh):
    grid = Mesh(mesh.devices.reshape(8, 4, 4, 2), ("z", "x", "y", "c"))
    lat, rep = ("z", "x"), REP
    tok = P(rep + lat, None)
    enc, dec = P(rep, lat), P(lat, rep)
    return jax.shard_map(
        local,
        mesh=grid,
        in_specs=(tok, tok, P(lat), enc, dec, enc, enc, dec, dec),
        out_specs=(enc, dec, enc, enc, dec, dec),
        check_vma=False,
    )
```

```python
import jax
import jax.numpy as jnp
from jax import lax
from jax.experimental import pallas as pl
from jax.experimental.pallas import tpu as pltpu
from jax.sharding import Mesh, PartitionSpec as P

BLOCK = 64
CAP = 5
LANES = 128
HOMES = 16
VMEM = 56 * 2**20

learn_rate = 0.001
adam_eps = 1e-08
first_fix = 1.0 - 0.9**10
second_fix = 1.0 - 0.95**10

REP = ("y", "c")
CHIPS = ("y", "x")


def adam(master, gradient, first, second):
    first_new = 0.9 * first + 0.1 * gradient
    second_new = 0.95 * second + 0.05 * gradient * gradient
    update = first_new / first_fix / (jnp.sqrt(second_new / second_fix) + adam_eps)
    return (master - learn_rate * update, first_new, second_new)


def dot(a, b, ca, cb):
    return lax.dot_general(a, b, (((ca,), (cb,)), ((), ())), preferred_element_type=jnp.float32)


def low_lanes(shape):
    return lax.broadcasted_iota(jnp.int32, shape, 1) < BLOCK


def split_pair(pair):
    low = low_lanes(pair.shape)
    zero = jnp.zeros_like(pair)
    return jnp.concatenate([jnp.where(low, pair, zero), jnp.where(low, zero, pair)], axis=0)


def join_pair(both):
    half = both.shape[0] // 2
    return jnp.where(low_lanes((half, LANES)), both[:half], both[half:])


def gather_onehot(pos_ref, home, slot, blocks, tok):
    rows = lax.broadcasted_iota(jnp.int32, (blocks, tok), 0) + slot * blocks
    first, second = pos_ref[home, 0:1, :], pos_ref[home, 1:2, :]
    return jnp.where((rows == first) | (rows == second), 1.0, 0.0).astype(jnp.bfloat16)


def scatter_onehot(col_ref, home, slot, blocks, tok):
    cols = lax.broadcasted_iota(jnp.int32, (tok, blocks), 1) + slot * blocks
    first, second = col_ref[home, :, 0:1], col_ref[home, :, 1:2]
    return jnp.where((cols == first) | (cols == second), 1.0, 0.0).astype(jnp.bfloat16)


def encode_kernel(tok_ref, pos_ref, enc_ref, pre_ref, rows_ref, held):
    tok = tok_ref.shape[0] // HOMES
    blocks = enc_ref.shape[0] // BLOCK
    per = CAP * HOMES

    @pl.loop(0, HOMES)
    def _(home):
        mine = tok_ref[pl.ds(pl.multiple_of(home * tok, tok), tok), :]
        for slot in range(CAP):
            picked = dot(gather_onehot(pos_ref, home, slot, blocks, tok), mine, 1, 0)
            held[pl.ds(slot * HOMES + home, blocks, per), :] = picked

    @pl.loop(0, blocks // 2, unroll=4)
    def _(pair):
        both = pl.ds(pl.multiple_of(pair * 2 * per, 2 * per), 2 * per)
        rows = held[both, :].astype(jnp.bfloat16)
        rows_ref[both, :] = rows
        weight = enc_ref[pl.ds(pl.multiple_of(pair * LANES, LANES), LANES), :]
        out = join_pair(dot(rows, weight, 1, 1)).astype(jnp.bfloat16)
        pre_ref[pl.ds(pl.multiple_of(pair * per, per), per), :] = out


def decode_kernel(code_ref, dec_ref, tok_ref, pos_ref, col_ref, cgrad_ref, dgrad_ref, held):
    tok = tok_ref.shape[0] // HOMES
    blocks = dec_ref.shape[0] // BLOCK
    per = CAP * HOMES

    @pl.loop(0, blocks // 2, unroll=4)
    def _(pair):
        both = pl.ds(pl.multiple_of(pair * 2 * per, 2 * per), 2 * per)
        code = split_pair(code_ref[pl.ds(pl.multiple_of(pair * per, per), per), :])
        weight = dec_ref[pl.ds(pl.multiple_of(pair * LANES, LANES), LANES), :]
        held[both, :] = dot(code, weight, 1, 0)

    @pl.loop(0, HOMES)
    def _(home):
        mine = tok_ref[pl.ds(pl.multiple_of(home * tok, tok), tok), :]
        rebuilt = jnp.zeros((tok, LANES), jnp.float32)
        for slot in range(CAP):
            part = held[pl.ds(slot * HOMES + home, blocks, per), :].astype(jnp.bfloat16)
            rebuilt += dot(scatter_onehot(col_ref, home, slot, blocks, tok), part, 1, 0)
        err = (rebuilt - mine.astype(jnp.float32)).astype(jnp.bfloat16)
        for slot in range(CAP):
            picked = dot(gather_onehot(pos_ref, home, slot, blocks, tok), err, 1, 0)
            held[pl.ds(slot * HOMES + home, blocks, per), :] = picked

    @pl.loop(0, blocks // 2, unroll=4)
    def _(pair):
        both = pl.ds(pl.multiple_of(pair * 2 * per, 2 * per), 2 * per)
        own = pl.ds(pl.multiple_of(pair * per, per), per)
        lanes = pl.ds(pl.multiple_of(pair * LANES, LANES), LANES)
        err = held[both, :].astype(jnp.bfloat16)
        cgrad_ref[own, :] = join_pair(dot(err, dec_ref[lanes, :], 1, 1)).astype(jnp.bfloat16)
        dgrad_ref[lanes, :] = dot(split_pair(code_ref[own, :]), err, 0, 0).astype(jnp.bfloat16)


def enc_grad_kernel(pgrad_ref, rows_ref, egrad_ref):
    per = CAP * HOMES

    @pl.loop(0, pgrad_ref.shape[0] // per, unroll=4)
    def _(pair):
        both = pl.ds(pl.multiple_of(pair * 2 * per, 2 * per), 2 * per)
        own = pl.ds(pl.multiple_of(pair * per, per), per)
        lanes = pl.ds(pl.multiple_of(pair * LANES, LANES), LANES)
        out = dot(split_pair(pgrad_ref[own, :]), rows_ref[both, :], 0, 0)
        egrad_ref[lanes, :] = out.astype(jnp.bfloat16)


def call(kernel, outs, scratch, name, *args):
    whole = pl.BlockSpec(memory_space=pltpu.VMEM)
    return pl.pallas_call(
        kernel,
        out_shape=[jax.ShapeDtypeStruct(s, jnp.bfloat16) for s in outs],
        in_specs=[whole] * len(args),
        out_specs=[whole] * len(outs),
        scratch_shapes=scratch,
        compiler_params=pltpu.CompilerParams(vmem_limit_bytes=VMEM),
        name=name,
    )(*args)


def local(
    tokens,
    block_ids,
    enc_bias,
    enc_master,
    dec_master,
    enc_first,
    enc_second,
    dec_first,
    dec_second,
):
    nz, nx = lax.axis_size("z"), lax.axis_size("x")
    ny, nc = lax.axis_size("y"), lax.axis_size("c")
    tok, width = tokens.shape
    lat, part = dec_master.shape
    blocks = lat // BLOCK * nz * nx
    half = lat // nc
    me = lax.axis_index("y") * nx + lax.axis_index("x")

    def spread(w):
        w = w.reshape(nc, half, part)
        w = lax.all_to_all(w, "c", split_axis=0, concat_axis=2, tiled=True)
        w = w.reshape(half, nx, LANES)
        w = lax.all_to_all(w, "x", split_axis=1, concat_axis=0, tiled=True)
        return lax.all_gather(w.reshape(nx * half, LANES), ("z", "c"), axis=0, tiled=True)

    per_half = half // BLOCK
    local_b = block_ids % (nc * per_half)
    shard = block_ids // (nc * per_half)
    place = (
        ((shard // nx) * nc + local_b // per_half) * nx + shard % nx
    ) * per_half + local_b % per_half
    nums = jnp.arange(blocks, dtype=jnp.int32)[:, None]
    named = [nums == place[:, k][None, :] for k in range(2)]
    count = jnp.cumsum((named[0] | named[1]).astype(jnp.int32), axis=1) - 1
    rank = jnp.stack([jnp.sum(jnp.where(n, count, 0), axis=0) for n in named])
    pos = lax.all_gather(rank * blocks + place.T, CHIPS, axis=0)
    col = pos.transpose(0, 2, 1)

    slices = tokens.reshape(tok, HOMES, LANES).transpose(1, 0, 2)
    slices = lax.all_to_all(slices, CHIPS, split_axis=0, concat_axis=0, tiled=True)
    slices = slices.reshape(HOMES * tok, LANES)

    enc = spread(enc_master.astype(jnp.bfloat16).T)
    dec = spread(dec_master.astype(jnp.bfloat16))
    bias = lax.all_gather(enc_bias, ("z", "x"), axis=0, tiled=True)
    bias = bias.reshape(nz, nx, nc, half).transpose(0, 2, 1, 3).reshape(HOMES, -1, 1, LANES)
    bias = lax.dynamic_index_in_dim(bias, me, 0, keepdims=False)

    per = CAP * HOMES
    codes = (blocks // 2 * per, LANES)
    held = [pltpu.VMEM((blocks * per, LANES), jnp.float32)]
    pre, rows = call(encode_kernel, [codes, (blocks * per, LANES)], held, "encode", slices, pos, enc)

    def reduce_own(partial):
        got = lax.all_to_all(
            partial.reshape(HOMES, -1, per, LANES), CHIPS, split_axis=0, concat_axis=0, tiled=True
        )
        return jnp.sum(got.astype(jnp.float32), axis=0)

    def share(own):
        return lax.all_gather(own, CHIPS, axis=0, tiled=True).reshape(codes)

    preact = reduce_own(pre) + bias
    values, slopes = jax.jvp(
        lambda inner: jax.nn.gelu(inner, approximate=True), (preact,), (jnp.ones_like(preact),)
    )
    coded = share(values.astype(jnp.bfloat16))
    cgrad, dgrad = call(
        decode_kernel,
        [codes, (blocks * BLOCK, LANES)],
        held,
        "decode",
        coded,
        dec,
        slices,
        pos,
        col,
    )
    pgrad = share((reduce_own(cgrad) * slopes).astype(jnp.bfloat16))
    (egrad,) = call(enc_grad_kernel, [(blocks * BLOCK, LANES)], [], "enc_grad", pgrad, rows)

    def collect(g):
        g = g.reshape(nz, nc, nx * half, LANES)
        g = lax.all_to_all(g, "c", split_axis=1, concat_axis=0, tiled=True).reshape(
            nc, nz, nx * half, LANES
        )
        g = jnp.sum(g.astype(jnp.float32), axis=0).astype(jnp.bfloat16)
        g = lax.all_to_all(g, "z", split_axis=0, concat_axis=0, tiled=True)
        g = jnp.sum(g.astype(jnp.float32), axis=0).reshape(nx, half, LANES)
        g = lax.all_to_all(g, "x", split_axis=0, concat_axis=2, tiled=True)
        g = g.reshape(1, half, nc, part)
        g = lax.all_to_all(g, "c", split_axis=2, concat_axis=0, tiled=True)
        return g.reshape(lat, part)

    dec_share = collect(dgrad)
    enc_share = collect(egrad).T
    enc_new, enc_first_new, enc_second_new = adam(enc_master, enc_share, enc_first, enc_second)
    dec_new, dec_first_new, dec_second_new = adam(dec_master, dec_share, dec_first, dec_second)
    return (enc_new, dec_new, enc_first_new, enc_second_new, dec_first_new, dec_second_new)


def solution(mesh):
    grid = Mesh(mesh.devices.reshape(8, 4, 4, 2), ("z", "x", "y", "c"))
    lat, rep = ("z", "x"), REP
    tok = P(rep + lat, None)
    enc, dec = P(rep, lat), P(lat, rep)
    return jax.shard_map(
        local,
        mesh=grid,
        in_specs=(tok, tok, P(lat), enc, dec, enc, enc, dec, dec),
        out_specs=(enc, dec, enc, enc, dec, dec),
        check_vma=False,
    )
```

```python
import jax
import jax.numpy as jnp
from jax import lax
from jax.experimental import pallas as pl
from jax.experimental.pallas import tpu as pltpu
from jax.sharding import Mesh, PartitionSpec as P

BLOCK = 64
CAP = 5
LANES = 128
HOMES = 16
VMEM = 56 * 2**20

learn_rate = 0.001
adam_eps = 1e-08
first_fix = 1.0 - 0.9**10
second_fix = 1.0 - 0.95**10

REP = ("y", "c")
CHIPS = ("y", "x")


def adam(master, gradient, first, second):
    first_new = 0.9 * first + 0.1 * gradient
    second_new = 0.95 * second + 0.05 * gradient * gradient
    update = first_new / first_fix / (jnp.sqrt(second_new / second_fix) + adam_eps)
    return (master - learn_rate * update, first_new, second_new)


def dot(a, b, ca, cb):
    return lax.dot_general(a, b, (((ca,), (cb,)), ((), ())), preferred_element_type=jnp.float32)


def low_lanes(shape):
    return lax.broadcasted_iota(jnp.int32, shape, 1) < BLOCK


def split_pair(pair):
    low = low_lanes(pair.shape)
    zero = jnp.zeros_like(pair)
    return jnp.concatenate([jnp.where(low, pair, zero), jnp.where(low, zero, pair)], axis=0)


def join_pair(both):
    half = both.shape[0] // 2
    return jnp.where(low_lanes((half, LANES)), both[:half], both[half:])


def gather_onehot(pos_ref, home, slot, blocks, tok):
    rows = lax.broadcasted_iota(jnp.int32, (blocks, tok), 0) + slot * blocks
    first, second = pos_ref[home, 0:1, :], pos_ref[home, 1:2, :]
    return jnp.where((rows == first) | (rows == second), 1.0, 0.0).astype(jnp.bfloat16)


def scatter_onehot(col_ref, home, slot, blocks, tok):
    cols = lax.broadcasted_iota(jnp.int32, (tok, blocks), 1) + slot * blocks
    first, second = col_ref[home, :, 0:1], col_ref[home, :, 1:2]
    return jnp.where((cols == first) | (cols == second), 1.0, 0.0).astype(jnp.bfloat16)


def encode_kernel(tok_ref, pos_ref, enc_ref, pre_ref, rows_ref, held):
    tok = tok_ref.shape[0] // HOMES
    blocks = enc_ref.shape[0] // BLOCK
    per = CAP * HOMES

    @pl.loop(0, HOMES)
    def _(home):
        mine = tok_ref[pl.ds(pl.multiple_of(home * tok, tok), tok), :]
        for slot in range(CAP):
            picked = dot(gather_onehot(pos_ref, home, slot, blocks, tok), mine, 1, 0)
            held[pl.ds(slot * HOMES + home, blocks, per), :] = picked

    @pl.loop(0, blocks // 2, unroll=4)
    def _(pair):
        both = pl.ds(pl.multiple_of(pair * 2 * per, 2 * per), 2 * per)
        rows = held[both, :].astype(jnp.bfloat16)
        rows_ref[both, :] = rows
        weight = enc_ref[pl.ds(pl.multiple_of(pair * LANES, LANES), LANES), :]
        out = join_pair(dot(rows, weight, 1, 1)).astype(jnp.bfloat16)
        pre_ref[pl.ds(pl.multiple_of(pair * per, per), per), :] = out


def decode_kernel(code_ref, dec_ref, tok_ref, pos_ref, col_ref, cgrad_ref, dgrad_ref, held):
    tok = tok_ref.shape[0] // HOMES
    blocks = dec_ref.shape[0] // BLOCK
    per = CAP * HOMES

    @pl.loop(0, blocks // 2, unroll=4)
    def _(pair):
        both = pl.ds(pl.multiple_of(pair * 2 * per, 2 * per), 2 * per)
        code = split_pair(code_ref[pl.ds(pl.multiple_of(pair * per, per), per), :])
        weight = dec_ref[pl.ds(pl.multiple_of(pair * LANES, LANES), LANES), :]
        held[both, :] = dot(code, weight, 1, 0)

    @pl.loop(0, HOMES)
    def _(home):
        mine = tok_ref[pl.ds(pl.multiple_of(home * tok, tok), tok), :]
        rebuilt = jnp.zeros((tok, LANES), jnp.float32)
        for slot in range(CAP):
            part = held[pl.ds(slot * HOMES + home, blocks, per), :].astype(jnp.bfloat16)
            rebuilt += dot(scatter_onehot(col_ref, home, slot, blocks, tok), part, 1, 0)
        err = (rebuilt - mine.astype(jnp.float32)).astype(jnp.bfloat16)
        for slot in range(CAP):
            picked = dot(gather_onehot(pos_ref, home, slot, blocks, tok), err, 1, 0)
            held[pl.ds(slot * HOMES + home, blocks, per), :] = picked

    @pl.loop(0, blocks // 2, unroll=4)
    def _(pair):
        both = pl.ds(pl.multiple_of(pair * 2 * per, 2 * per), 2 * per)
        own = pl.ds(pl.multiple_of(pair * per, per), per)
        lanes = pl.ds(pl.multiple_of(pair * LANES, LANES), LANES)
        err = held[both, :].astype(jnp.bfloat16)
        cgrad_ref[own, :] = join_pair(dot(err, dec_ref[lanes, :], 1, 1)).astype(jnp.bfloat16)
        dgrad_ref[lanes, :] = dot(split_pair(code_ref[own, :]), err, 0, 0)


def enc_grad_kernel(pgrad_ref, rows_ref, egrad_ref):
    per = CAP * HOMES

    @pl.loop(0, pgrad_ref.shape[0] // per, unroll=4)
    def _(pair):
        both = pl.ds(pl.multiple_of(pair * 2 * per, 2 * per), 2 * per)
        own = pl.ds(pl.multiple_of(pair * per, per), per)
        lanes = pl.ds(pl.multiple_of(pair * LANES, LANES), LANES)
        egrad_ref[lanes, :] = dot(split_pair(pgrad_ref[own, :]), rows_ref[both, :], 0, 0)


def call(kernel, outs, scratch, name, *args):
    whole = pl.BlockSpec(memory_space=pltpu.VMEM)
    return pl.pallas_call(
        kernel,
        out_shape=[jax.ShapeDtypeStruct(s, t) for s, t in outs],
        in_specs=[whole] * len(args),
        out_specs=[whole] * len(outs),
        scratch_shapes=scratch,
        compiler_params=pltpu.CompilerParams(vmem_limit_bytes=VMEM),
        name=name,
    )(*args)


MESH = pl.DeviceIdType.MESH


def axis_ids():
    return {a: lax.axis_index(a) for a in ("z", "x", "y", "c")}


def step(ids, axis, d):
    n = lax.axis_size(axis)
    return lax.rem(ids[axis] + (d + n), n)


def meet(peers):
    barrier = pltpu.get_barrier_semaphore()
    for peer in peers:
        pl.semaphore_signal(barrier, inc=1, device_id=peer, device_id_type=MESH)
    pl.semaphore_wait(barrier, len(peers))


def send(src, dst, ssem, rsem, peer):
    copy = pltpu.make_async_remote_copy(
        src_ref=src, dst_ref=dst, send_sem=ssem, recv_sem=rsem, device_id=peer, device_id_type=MESH
    )
    copy.start()
    return copy


def finish(copies):
    for copy in copies:
        copy.wait()


def ring_peers(ids, axis):
    return [{axis: step(ids, axis, d)} for d in range(1, lax.axis_size(axis))]


def reduce_share(ids, part, out, first, second, total, ssem, rsem, middle):
    x, y = ids["x"], ids["y"]
    half = part.shape[2] // 2
    top, low = pl.ds(0, half), pl.ds(half, half)

    def stage(k, pairs):
        copies = []
        for d in (1, 3, 2):
            for h in range(2):
                src, dst, peer = pairs(h, d)
                copies.append(send(src, dst, ssem.at[k, h, d - 1], rsem.at[k, h, d - 1], peer))
        return copies

    def one(h, d):
        if h == 0:
            t = step(ids, "x", d)
            return part.at[:, t, top], first.at[0, d - 1], {"x": t}
        t = step(ids, "y", d)
        return part.at[t, :, low], first.at[1, d - 1], {"y": t}

    finish(stage(0, one))
    for k in range(4):
        for h, own in ((0, part.at[k, x, top]), (1, part.at[y, k, low])):
            acc = own[...].astype(jnp.float32)
            for d in range(3):
                acc += first[h, d, k].astype(jnp.float32)
            total[h, k] = acc

    def two(h, d):
        axis = "y" if h == 0 else "x"
        t = step(ids, axis, d)
        return total.at[h, t], second.at[h, d - 1], {axis: t}

    finish(stage(1, two))
    for h, mine in ((0, y), (1, x)):
        acc = total[h, mine]
        for d in range(3):
            acc += second[h, d]
        middle(h, acc)

    def three(h, d):
        axis, rows = ("y", top) if h == 0 else ("x", low)
        return out.at[y, x, rows], out.at[y, x, rows], {axis: step(ids, axis, d)}

    finish(stage(2, three))

    def four(h, d):
        if h == 0:
            return out.at[:, x, top], out.at[:, x, top], {"x": step(ids, "x", d)}
        return out.at[y, :, low], out.at[y, :, low], {"y": step(ids, "y", d)}

    return stage(3, four)


def gelu_parts(v):
    a, b = 0.7978845608028654, 0.044715
    t = jnp.tanh(a * (v + b * (v * v * v)))
    value = 0.5 * v * (1.0 + t)
    slope = 0.5 * (1.0 + t) + 0.5 * v * (1.0 - t * t) * (a * (1.0 + 3.0 * b * (v * v)))
    return value, slope


def code_kernel(
    part, bias, dec_own, out, slopes, dec, first, second, total, ssem, rsem, zsend, zrecv, csend, crecv, lsem
):
    ids = axis_ids()
    x, y, z, c = ids["x"], ids["y"], ids["z"], ids["c"]
    other = {"c": 1 - c}
    meet(ring_peers(ids, "x") + ring_peers(ids, "y") + ring_peers(ids, "z") + [other])
    mine = pltpu.make_async_copy(dec_own, dec.at[z, c], lsem)
    mine.start()
    around = [
        send(dec_own, dec.at[z, c], zsend.at[d - 1], zrecv.at[d - 1], {"z": step(ids, "z", d)})
        for d in (1, 7, 2, 6, 3, 5, 4)
    ]
    half = part.shape[2] // 2

    def middle(h, acc):
        at = pl.ds(h * half, half)
        value, slope = gelu_parts(acc + bias[at, :])
        out[y, x, at] = value.astype(jnp.bfloat16)
        slopes[at, :] = slope

    last = reduce_share(ids, part, out, first, second, total, ssem, rsem, middle)
    mine.wait()
    finish(around)
    over = send(dec.at[:, c], dec.at[:, c], csend, crecv, other)
    finish(last)
    over.wait()


def grad_kernel(part, slopes, out, first, second, total, ssem, rsem):
    ids = axis_ids()
    meet(ring_peers(ids, "x") + ring_peers(ids, "y"))
    half = part.shape[2] // 2

    def middle(h, acc):
        at = pl.ds(h * half, half)
        out[ids["y"], ids["x"], at] = (acc * slopes[at, :]).astype(jnp.bfloat16)

    finish(reduce_share(ids, part, out, first, second, total, ssem, rsem, middle))


def home_peers(ids):
    return [
        {"x": step(ids, "x", d), "c": lax.rem(ids["c"] + e, 2)}
        for d in range(4)
        for e in range(2)
        if (d, e) != (0, 0)
    ]


def spread_kernel(
    slices, pos, enc, dec, tok_all, pos_all, enc_all, dec_own, tsend, trecv, psend, precv,
    wsend, wrecv, rsend, rrecv, csend, crecv, lsem,
):
    ids = axis_ids()
    x, y, z, c = ids["x"], ids["y"], ids["z"], ids["c"]
    plane = [(a, b) for a, b in (
        (1, 0), (0, 1), (3, 0), (0, 3), (1, 1), (3, 3), (1, 3), (3, 1),
        (2, 0), (0, 2), (1, 2), (2, 1), (3, 2), (2, 3), (2, 2),
    )]
    peers = [{"y": step(ids, "y", a), "x": step(ids, "x", b)} for a, b in plane]
    crossed = [{"x": step(ids, "x", d), "c": 1 - c} for d in range(4)]
    meet(peers + crossed + [{"z": step(ids, "z", 1)}, {"z": step(ids, "z", -1)}])

    here = []
    lat = enc.shape[0] // 2

    swap = []
    for m, w in enumerate((enc, dec)):
        for i in range(2):
            for h in range(2):
                t = 2 * c + i
                src = w.at[pl.ds(h * lat, lat), pl.ds(i * LANES, LANES)]
                at = pl.ds(pl.multiple_of(x * lat, lat), lat)
                dst = enc_all.at[z, h, at] if m == 0 else dec_own.at[at]
                own = (t == x) & (c == h)
                copy = pltpu.make_async_remote_copy(
                    src_ref=src, dst_ref=dst, send_sem=wsend.at[m, i, h], recv_sem=wrecv.at[m, x],
                    device_id={"x": t, "c": h}, device_id_type=MESH,
                )
                keep = pltpu.make_async_copy(src, dst, wrecv.at[m, x])

                @pl.when(own)
                def _():
                    keep.start()

                @pl.when(jnp.logical_not(own))
                def _():
                    copy.start()

                swap.append((own, copy))

    for n, (a, b) in enumerate(plane):
        t = step(ids, "y", a) * 4 + step(ids, "x", b)
        me = y * 4 + x
        here.append(send(pos, pos_all.at[me], psend.at[n], precv.at[n], peers[n]))
        here.append(send(slices.at[t], tok_all.at[me], tsend.at[n], trecv.at[n], peers[n]))
    me = y * 4 + x
    keep_pos = pltpu.make_async_copy(pos, pos_all.at[me], lsem.at[0])
    keep_tok = pltpu.make_async_copy(slices.at[me], tok_all.at[me], lsem.at[1])
    keep_pos.start()
    keep_tok.start()

    def arrived(m, src):
        at = pl.ds(src * lat, lat)
        dst = enc_all.at[z, c, at] if m == 0 else dec_own.at[at]
        pltpu.make_async_copy(dst, dst, wrecv.at[m, src]).wait()

    for src in range(4):
        arrived(0, src)
    other = {"c": 1 - c}
    right, left = {"z": step(ids, "z", 1)}, {"z": step(ids, "z", -1)}

    def block(zz):
        return enc_all.at[zz, c]

    ring, over = [], []
    over.append(send(block(z), block(z), csend.at[0], crecv.at[0], other))
    ups = [send(block(z), block(z), rsend.at[0, 0], rrecv.at[0, 0], right)]
    downs = [send(block(z), block(z), rsend.at[1, 0], rrecv.at[1, 0], left)]
    for k in range(1, 5):
        zz = step(ids, "z", -k)
        ups[k - 1].wait_recv()
        if k < 4:
            ups.append(send(block(zz), block(zz), rsend.at[0, k], rrecv.at[0, k], right))
        over.append(send(block(zz), block(zz), csend.at[k], crecv.at[k], other))
        if k < 4:
            zz = step(ids, "z", k)
            downs[k - 1].wait_recv()
            if k < 3:
                downs.append(send(block(zz), block(zz), rsend.at[1, k], rrecv.at[1, k], left))
            over.append(send(block(zz), block(zz), csend.at[4 + k], crecv.at[4 + k], other))
    for copy in ups + downs:
        copy.wait_send()
    finish(over)
    keep_pos.wait()
    keep_tok.wait()
    for src in range(4):
        arrived(1, src)
    for own, copy in swap:
        @pl.when(jnp.logical_not(own))
        def _():
            copy.wait_send()
    finish(here)


def collect_kernel(
    enc, dec, enc_out, dec_out, half_in, narrow, z_in, total, csend, crecv, zsend, zrecv, hsend, hrecv,
):
    ids = axis_ids()
    x, z, c = ids["x"], ids["z"], ids["c"]
    other = {"c": 1 - c}
    meet(ring_peers(ids, "z") + home_peers(ids))
    nz = lax.axis_size("z")
    both = ((0, dec, dec_out), (1, enc, enc_out))
    swaps = [send(g.at[:, 1 - c], half_in.at[m], csend.at[m], crecv.at[m], other) for m, g, _ in both]
    around = []
    for m, g, _ in both:
        swaps[m].wait()
        for d in (1, 7, 2, 6, 3, 5, 4, 0):
            t = step(ids, "z", d)
            acc = g[t, c].astype(jnp.float32) + half_in[m, t].astype(jnp.float32)
            if d == 0:
                total[m] = acc
                continue
            narrow[m, t] = acc.astype(jnp.bfloat16)
            around.append(
                send(narrow.at[m, t], z_in.at[m, d - 1], zsend.at[m, d - 1], zrecv.at[m, d - 1], {"z": t})
            )
    lat = dec_out.shape[0] // 2
    owner_c = x // 2
    lanes = pl.ds(pl.multiple_of(lax.rem(x, 2) * LANES, LANES), LANES)
    rows = pl.ds(pl.multiple_of(c * lat, lat), lat)
    homes = []
    for m, _, out in both:
        finish(around[m * 7 : m * 7 + 7])
        total[m] += sum(z_in[m, d].astype(jnp.float32) for d in range(nz - 1))
        for t in range(4):
            src, dst = total.at[m, pl.ds(t * lat, lat)], out.at[rows, lanes]
            own = (t == x) & (owner_c == c)
            sem = hrecv.at[m, c, lax.rem(x, 2)]
            copy = pltpu.make_async_remote_copy(
                src_ref=src, dst_ref=dst, send_sem=hsend.at[m, t], recv_sem=sem,
                device_id={"x": t, "c": owner_c}, device_id_type=MESH,
            )
            keep = pltpu.make_async_copy(src, dst, sem)

            @pl.when(own)
            def _():
                keep.start()

            @pl.when(jnp.logical_not(own))
            def _():
                copy.start()

            homes.append((own, copy))
    for m, _, out in both:
        for h in range(2):
            for i in range(2):
                dst = out.at[pl.ds(h * lat, lat), pl.ds(i * LANES, LANES)]
                pltpu.make_async_copy(dst, dst, hrecv.at[m, h, i]).wait()
    for own, copy in homes:
        @pl.when(jnp.logical_not(own))
        def _():
            copy.wait_send()


def talk(kernel, outs, scratch, cid, *args):
    whole = pl.BlockSpec(memory_space=pltpu.VMEM)
    return pl.pallas_call(
        kernel,
        out_shape=[jax.ShapeDtypeStruct(s, t) for s, t in outs],
        in_specs=[whole] * len(args),
        out_specs=[whole] * len(outs),
        scratch_shapes=scratch,
        compiler_params=pltpu.CompilerParams(
            collective_id=cid, has_side_effects=True, vmem_limit_bytes=VMEM
        ),
        name=kernel.__name__,
    )(*args)


def sems(*shape):
    return pltpu.SemaphoreType.DMA(shape)


def local(
    tokens,
    block_ids,
    enc_bias,
    enc_master,
    dec_master,
    enc_first,
    enc_second,
    dec_first,
    dec_second,
):
    nz, nx = lax.axis_size("z"), lax.axis_size("x")
    ny, nc = lax.axis_size("y"), lax.axis_size("c")
    tok, width = tokens.shape
    lat, part = dec_master.shape
    blocks = lat // BLOCK * nz * nx
    half = lat // nc
    me = lax.axis_index("y") * nx + lax.axis_index("x")

    per_half = half // BLOCK
    local_b = block_ids % (nc * per_half)
    shard = block_ids // (nc * per_half)
    place = (
        ((shard // nx) * nc + local_b // per_half) * nx + shard % nx
    ) * per_half + local_b % per_half
    nums = jnp.arange(blocks, dtype=jnp.int32)[:, None]
    named = [nums == place[:, k][None, :] for k in range(2)]
    count = jnp.cumsum((named[0] | named[1]).astype(jnp.int32), axis=1) - 1
    rank = jnp.stack([jnp.sum(jnp.where(n, count, 0), axis=0) for n in named])
    pos = jnp.pad(rank * blocks + place.T, ((0, 6), (0, 0)))

    bf, f32 = jnp.bfloat16, jnp.float32
    per = CAP * HOMES
    rows_own = blocks // 2 // HOMES * per
    slices = tokens.reshape(tok, HOMES, LANES).transpose(1, 0, 2)
    own_w = nx * half
    slices, pos, enc, dec_own = talk(
        spread_kernel,
        [
            ((HOMES, tok, LANES), bf),
            ((HOMES, 8, tok), jnp.int32),
            ((nz, nc, own_w, LANES), bf),
            ((own_w, LANES), bf),
        ],
        [sems(15), sems(15), sems(15), sems(15), sems(2, 2, 2), sems(2, 4), sems(2, 4), sems(2, 4),
         sems(8), sems(8), sems(2)],
        1,
        slices,
        pos,
        enc_master.astype(bf).T,
        dec_master.astype(bf),
    )
    slices = slices.reshape(HOMES * tok, LANES)
    col = pos[:, :2].transpose(0, 2, 1)
    enc = enc.reshape(-1, LANES)
    bias = lax.all_gather(enc_bias, ("z", "x"), axis=0, tiled=True)
    bias = bias.reshape(nz, nx, nc, half).transpose(0, 2, 1, 3).reshape(HOMES, -1, 1, LANES)
    bias = lax.dynamic_index_in_dim(bias, me, 0, keepdims=False)
    bias = jnp.broadcast_to(bias, (bias.shape[0], per, LANES)).reshape(rows_own, LANES)

    codes = (blocks // 2 * per, LANES)
    grid4 = (ny, nx, rows_own, LANES)
    held = [pltpu.VMEM((blocks * per, LANES), f32)]
    stages = [
        pltpu.VMEM((2, 3, 4, rows_own // 2, LANES), bf),
        pltpu.VMEM((2, 3, rows_own // 2, LANES), f32),
        pltpu.VMEM((2, 4, rows_own // 2, LANES), f32),
        sems(4, 2, 3),
        sems(4, 2, 3),
    ]
    pre, rows = call(encode_kernel, [(codes, bf), ((blocks * per, LANES), bf)], held, "encode", slices, pos, enc)
    coded, slopes, dec = talk(
        code_kernel,
        [(grid4, bf), ((rows_own, LANES), f32), ((nz, nc, own_w, LANES), bf)],
        stages + [sems(7), sems(7), pltpu.SemaphoreType.DMA, pltpu.SemaphoreType.DMA, pltpu.SemaphoreType.DMA],
        2,
        pre.reshape(grid4),
        bias,
        dec_own,
    )
    cgrad, dgrad = call(
        decode_kernel,
        [(codes, bf), ((blocks * BLOCK, LANES), f32)],
        held,
        "decode",
        coded.reshape(codes),
        dec.reshape(-1, LANES),
        slices,
        pos,
        col,
    )
    (pgrad,) = talk(grad_kernel, [(grid4, bf)], stages, 3, cgrad.reshape(grid4), slopes)
    (egrad,) = call(enc_grad_kernel, [((blocks * BLOCK, LANES), f32)], [], "enc_grad", pgrad.reshape(codes), rows)
    grads = (nz, nc, own_w, LANES)
    enc_share, dec_share = talk(
        collect_kernel,
        [((lat, part), f32), ((lat, part), f32)],
        [
            pltpu.VMEM((2, nz, own_w, LANES), f32),
            pltpu.VMEM((2, nz, own_w, LANES), bf),
            pltpu.VMEM((2, nz - 1, own_w, LANES), bf),
            pltpu.VMEM((2, own_w, LANES), f32),
            sems(2), sems(2), sems(2, 7), sems(2, 7), sems(2, 4), sems(2, 2, 2),
        ],
        4,
        egrad.reshape(grads),
        dgrad.reshape(grads),
    )
    enc_share = enc_share.T
    enc_new, enc_first_new, enc_second_new = adam(enc_master, enc_share, enc_first, enc_second)
    dec_new, dec_first_new, dec_second_new = adam(dec_master, dec_share, dec_first, dec_second)
    return (enc_new, dec_new, enc_first_new, enc_second_new, dec_first_new, dec_second_new)


def solution(mesh):
    grid = Mesh(mesh.devices.reshape(8, 4, 4, 2), ("z", "x", "y", "c"))
    lat, rep = ("z", "x"), REP
    tok = P(rep + lat, None)
    enc, dec = P(rep, lat), P(lat, rep)
    return jax.shard_map(
        local,
        mesh=grid,
        in_specs=(tok, tok, P(lat), enc, dec, enc, enc, dec, dec),
        out_specs=(enc, dec, enc, enc, dec, dec),
        check_vma=False,
    )
```

```python
import jax
import jax.numpy as jnp
from jax import lax
from jax.experimental import pallas as pl
from jax.experimental.pallas import tpu as pltpu
from jax.sharding import Mesh, PartitionSpec as P

BLOCK = 64
CAP = 5
LANES = 128
HOMES = 16
VMEM = 56 * 2**20

learn_rate = 0.001
adam_eps = 1e-08
first_fix = 1.0 - 0.9**10
second_fix = 1.0 - 0.95**10

REP = ("y", "c")
CHIPS = ("y", "x")


def adam(master, gradient, first, second):
    first_new = 0.9 * first + 0.1 * gradient
    second_new = 0.95 * second + 0.05 * gradient * gradient
    update = first_new / first_fix / (jnp.sqrt(second_new / second_fix) + adam_eps)
    return (master - learn_rate * update, first_new, second_new)


def dot(a, b, ca, cb):
    return lax.dot_general(a, b, (((ca,), (cb,)), ((), ())), preferred_element_type=jnp.float32)


def low_lanes(shape):
    return lax.broadcasted_iota(jnp.int32, shape, 1) < BLOCK


def split_pair(pair):
    low = low_lanes(pair.shape)
    zero = jnp.zeros_like(pair)
    return jnp.concatenate([jnp.where(low, pair, zero), jnp.where(low, zero, pair)], axis=0)


def join_pair(both):
    half = both.shape[0] // 2
    return jnp.where(low_lanes((half, LANES)), both[:half], both[half:])


def slot_onehot(pos_ref, home, slot, blocks, tok):
    rows = (lax.broadcasted_iota(jnp.int32, (blocks, tok), 0) + slot * blocks).astype(jnp.int16)
    first = pos_ref[home, 0:1, :].astype(jnp.int16)
    second = pos_ref[home, 1:2, :].astype(jnp.int16)
    one, zero = jnp.ones((), jnp.bfloat16), jnp.zeros((), jnp.bfloat16)
    return jnp.where((rows == first) | (rows == second), one, zero)


def encode_kernel(tok_ref, pos_ref, enc_ref, pre_ref, rows_ref, held):
    tok = tok_ref.shape[0] // HOMES
    blocks = enc_ref.shape[0] // BLOCK
    per = CAP * HOMES

    @pl.loop(0, HOMES)
    def _(home):
        mine = tok_ref[pl.ds(pl.multiple_of(home * tok, tok), tok), :]
        for slot in range(CAP):
            picked = dot(slot_onehot(pos_ref, home, slot, blocks, tok), mine, 1, 0)
            held[pl.ds(slot * HOMES + home, blocks, per), :] = picked

    @pl.loop(0, blocks // 2, unroll=8)
    def _(pair):
        both = pl.ds(pl.multiple_of(pair * 2 * per, 2 * per), 2 * per)
        rows = held[both, :].astype(jnp.bfloat16)
        rows_ref[both, :] = rows
        weight = enc_ref[pl.ds(pl.multiple_of(pair * LANES, LANES), LANES), :]
        out = join_pair(dot(rows, weight, 1, 1)).astype(jnp.bfloat16)
        pre_ref[pl.ds(pl.multiple_of(pair * per, per), per), :] = out


def decode_kernel(code_ref, dec_ref, tok_ref, pos_ref, cgrad_ref, dgrad_ref, held):
    tok = tok_ref.shape[0] // HOMES
    blocks = dec_ref.shape[0] // BLOCK
    per = CAP * HOMES

    @pl.loop(0, blocks // 2, unroll=8)
    def _(pair):
        both = pl.ds(pl.multiple_of(pair * 2 * per, 2 * per), 2 * per)
        code = split_pair(code_ref[pl.ds(pl.multiple_of(pair * per, per), per), :])
        weight = dec_ref[pl.ds(pl.multiple_of(pair * LANES, LANES), LANES), :]
        held[both, :] = dot(code, weight, 1, 0)

    @pl.loop(0, HOMES)
    def _(home):
        mine = tok_ref[pl.ds(pl.multiple_of(home * tok, tok), tok), :]
        rebuilt = jnp.zeros((tok, LANES), jnp.float32)
        for slot in range(CAP):
            part = held[pl.ds(slot * HOMES + home, blocks, per), :].astype(jnp.bfloat16)
            rebuilt += dot(slot_onehot(pos_ref, home, slot, blocks, tok), part, 0, 0)
        err = (rebuilt - mine.astype(jnp.float32)).astype(jnp.bfloat16)
        for slot in range(CAP):
            picked = dot(slot_onehot(pos_ref, home, slot, blocks, tok), err, 1, 0)
            held[pl.ds(slot * HOMES + home, blocks, per), :] = picked

    @pl.loop(0, blocks // 2, unroll=8)
    def _(pair):
        both = pl.ds(pl.multiple_of(pair * 2 * per, 2 * per), 2 * per)
        own = pl.ds(pl.multiple_of(pair * per, per), per)
        lanes = pl.ds(pl.multiple_of(pair * LANES, LANES), LANES)
        err = held[both, :].astype(jnp.bfloat16)
        cgrad_ref[own, :] = join_pair(dot(err, dec_ref[lanes, :], 1, 1)).astype(jnp.bfloat16)
        dgrad_ref[lanes, :] = dot(split_pair(code_ref[own, :]), err, 0, 0)


def call(kernel, outs, scratch, name, *args):
    whole = pl.BlockSpec(memory_space=pltpu.VMEM)
    return pl.pallas_call(
        kernel,
        out_shape=[jax.ShapeDtypeStruct(s, t) for s, t in outs],
        in_specs=[whole] * len(args),
        out_specs=[whole] * len(outs),
        scratch_shapes=scratch,
        compiler_params=pltpu.CompilerParams(vmem_limit_bytes=VMEM),
        name=name,
    )(*args)


MESH = pl.DeviceIdType.MESH


def axis_ids():
    return {a: lax.axis_index(a) for a in ("z", "x", "y", "c")}


def step(ids, axis, d):
    n = lax.axis_size(axis)
    return lax.rem(ids[axis] + (d + n), n)


def meet(peers):
    barrier = pltpu.get_barrier_semaphore()
    for peer in peers:
        pl.semaphore_signal(barrier, inc=1, device_id=peer, device_id_type=MESH)
    pl.semaphore_wait(barrier, len(peers))


def send(src, dst, ssem, rsem, peer):
    copy = pltpu.make_async_remote_copy(
        src_ref=src, dst_ref=dst, send_sem=ssem, recv_sem=rsem, device_id=peer, device_id_type=MESH
    )
    copy.start()
    return copy


def finish(copies):
    for copy in copies:
        copy.wait()


def ring_peers(ids, axis):
    return [{axis: step(ids, axis, d)} for d in range(1, lax.axis_size(axis))]


def reduce_share(ids, part, out, first, second, total, ssem, rsem, middle, beside=None):
    x, y = ids["x"], ids["y"]
    half = part.shape[2] // 2
    top, low = pl.ds(0, half), pl.ds(half, half)

    def stage(k, pairs):
        copies = []
        for d in (1, 3, 2):
            for h in range(2):
                src, dst, peer = pairs(h, d)
                copies.append(send(src, dst, ssem.at[k, h, d - 1], rsem.at[k, h, d - 1], peer))
        return copies

    def one(h, d):
        if h == 0:
            t = step(ids, "x", d)
            return part.at[:, t, top], first.at[0, d - 1], {"x": t}
        t = step(ids, "y", d)
        return part.at[t, :, low], first.at[1, d - 1], {"y": t}

    copies = stage(0, one)
    if beside is not None:
        beside()
    finish(copies)
    for k in range(4):
        for h, own in ((0, part.at[k, x, top]), (1, part.at[y, k, low])):
            acc = own[...].astype(jnp.float32)
            for d in range(3):
                acc += first[h, d, k].astype(jnp.float32)
            total[h, k] = acc

    def two(h, d):
        axis = "y" if h == 0 else "x"
        t = step(ids, axis, d)
        return total.at[h, t], second.at[h, d - 1], {axis: t}

    finish(stage(1, two))
    for h, mine in ((0, y), (1, x)):
        acc = total[h, mine]
        for d in range(3):
            acc += second[h, d]
        middle(h, acc)

    def three(h, d):
        axis, rows = ("y", top) if h == 0 else ("x", low)
        return out.at[y, x, rows], out.at[y, x, rows], {axis: step(ids, axis, d)}

    finish(stage(2, three))

    def four(h, d):
        if h == 0:
            return out.at[:, x, top], out.at[:, x, top], {"x": step(ids, "x", d)}
        return out.at[y, :, low], out.at[y, :, low], {"y": step(ids, "y", d)}

    return stage(3, four)


def gelu_parts(v):
    a, b = 0.7978845608028654, 0.044715
    t = jnp.tanh(a * (v + b * (v * v * v)))
    value = 0.5 * v * (1.0 + t)
    slope = 0.5 * (1.0 + t) + 0.5 * v * (1.0 - t * t) * (a * (1.0 + 3.0 * b * (v * v)))
    return value, slope


def code_kernel(
    part, bias, dec_own, out, slopes, dec, first, second, total, ssem, rsem, zsend, zrecv, csend, crecv, lsem
):
    ids = axis_ids()
    x, y, z, c = ids["x"], ids["y"], ids["z"], ids["c"]
    other = {"c": 1 - c}
    meet(ring_peers(ids, "x") + ring_peers(ids, "y") + ring_peers(ids, "z") + [other])
    mine = pltpu.make_async_copy(dec_own, dec.at[z, c], lsem)
    mine.start()
    around = [
        send(dec_own, dec.at[z, c], zsend.at[d - 1], zrecv.at[d - 1], {"z": step(ids, "z", d)})
        for d in (1, 7, 2, 6, 3, 5, 4)
    ]
    half = part.shape[2] // 2

    def middle(h, acc):
        at = pl.ds(h * half, half)
        value, slope = gelu_parts(acc + bias[at, :])
        out[y, x, at] = value.astype(jnp.bfloat16)
        slopes[at, :] = slope

    last = reduce_share(ids, part, out, first, second, total, ssem, rsem, middle)
    mine.wait()
    finish(around)
    over = send(dec.at[:, c], dec.at[:, c], csend, crecv, other)
    finish(last)
    over.wait()


def home_peers(ids):
    return [
        {"x": step(ids, "x", d), "c": lax.rem(ids["c"] + e, 2)}
        for d in range(4)
        for e in range(2)
        if (d, e) != (0, 0)
    ]


def spread_kernel(
    slices, pos, enc, dec, bias, tok_all, pos_all, enc_all, dec_own, bias_all, tsend, trecv, psend, precv,
    wsend, wrecv, rsend, rrecv, csend, crecv, lsem, bsend, brecv, zsend, zrecv,
):
    ids = axis_ids()
    x, y, z, c = ids["x"], ids["y"], ids["z"], ids["c"]
    plane = [(a, b) for a, b in (
        (1, 0), (0, 1), (3, 0), (0, 3), (1, 1), (3, 3), (1, 3), (3, 1),
        (2, 0), (0, 2), (1, 2), (2, 1), (3, 2), (2, 3), (2, 2),
    )]
    peers = [{"y": step(ids, "y", a), "x": step(ids, "x", b)} for a, b in plane]
    crossed = [{"x": step(ids, "x", d), "c": 1 - c} for d in range(4)]
    meet(peers + crossed + ring_peers(ids, "z"))

    here = []
    bias_x = [
        send(bias, bias_all.at[z, x], bsend.at[d - 1], brecv.at[d - 1], {"x": step(ids, "x", d)})
        for d in range(1, 4)
    ]
    keep_bias = pltpu.make_async_copy(bias, bias_all.at[z, x], lsem.at[2])
    keep_bias.start()
    lat = enc.shape[0] // 2

    swap = []
    for m, w in enumerate((enc, dec)):
        for i in range(2):
            for h in range(2):
                t = 2 * c + i
                src = w.at[pl.ds(h * lat, lat), pl.ds(i * LANES, LANES)]
                at = pl.ds(pl.multiple_of(x * lat, lat), lat)
                dst = enc_all.at[z, h, at] if m == 0 else dec_own.at[at]
                own = (t == x) & (c == h)
                copy = pltpu.make_async_remote_copy(
                    src_ref=src, dst_ref=dst, send_sem=wsend.at[m, i, h], recv_sem=wrecv.at[m, x],
                    device_id={"x": t, "c": h}, device_id_type=MESH,
                )
                keep = pltpu.make_async_copy(src, dst, wrecv.at[m, x])

                @pl.when(own)
                def _():
                    keep.start()

                @pl.when(jnp.logical_not(own))
                def _():
                    copy.start()

                swap.append((own, copy))

    for n, (a, b) in enumerate(plane):
        t = step(ids, "y", a) * 4 + step(ids, "x", b)
        me = y * 4 + x
        here.append(send(pos, pos_all.at[me], psend.at[n], precv.at[n], peers[n]))
        here.append(send(slices.at[t], tok_all.at[me], tsend.at[n], trecv.at[n], peers[n]))
    me = y * 4 + x
    keep_pos = pltpu.make_async_copy(pos, pos_all.at[me], lsem.at[0])
    keep_tok = pltpu.make_async_copy(slices.at[me], tok_all.at[me], lsem.at[1])
    keep_pos.start()
    keep_tok.start()

    def arrived(m, src):
        at = pl.ds(src * lat, lat)
        dst = enc_all.at[z, c, at] if m == 0 else dec_own.at[at]
        pltpu.make_async_copy(dst, dst, wrecv.at[m, src]).wait()

    for src in range(4):
        arrived(0, src)
    other = {"c": 1 - c}
    finish(bias_x)
    keep_bias.wait()
    here += [
        send(bias_all.at[z], bias_all.at[z], zsend.at[d - 1], zrecv.at[d - 1], {"z": step(ids, "z", d)})
        for d in range(1, 8)
    ]
    right, left = {"z": step(ids, "z", 1)}, {"z": step(ids, "z", -1)}

    def block(zz):
        return enc_all.at[zz, c]

    ring, over = [], []
    over.append(send(block(z), block(z), csend.at[0], crecv.at[0], other))
    ups = [send(block(z), block(z), rsend.at[0, 0], rrecv.at[0, 0], right)]
    downs = [send(block(z), block(z), rsend.at[1, 0], rrecv.at[1, 0], left)]
    for k in range(1, 5):
        zz = step(ids, "z", -k)
        ups[k - 1].wait_recv()
        if k < 4:
            ups.append(send(block(zz), block(zz), rsend.at[0, k], rrecv.at[0, k], right))
        over.append(send(block(zz), block(zz), csend.at[k], crecv.at[k], other))
        if k < 4:
            zz = step(ids, "z", k)
            downs[k - 1].wait_recv()
            if k < 3:
                downs.append(send(block(zz), block(zz), rsend.at[1, k], rrecv.at[1, k], left))
            over.append(send(block(zz), block(zz), csend.at[4 + k], crecv.at[4 + k], other))
    for copy in ups + downs:
        copy.wait_send()
    finish(over)
    keep_pos.wait()
    keep_tok.wait()
    for src in range(4):
        arrived(1, src)
    for own, copy in swap:
        @pl.when(jnp.logical_not(own))
        def _():
            copy.wait_send()
    finish(here)


def tail_kernel(
    part, slopes, dec, rows, enc_out, dec_out, codes, first, second, total, ssem, rsem,
    enc, half_in, narrow, z_in, sums, csend, crecv, zsend, zrecv, hsend, hrecv,
):
    ids = axis_ids()
    x, y, z, c = ids["x"], ids["y"], ids["z"], ids["c"]
    other = {"c": 1 - c}
    meet(ring_peers(ids, "y") + ring_peers(ids, "z") + home_peers(ids))
    nz = lax.axis_size("z")
    half = part.shape[2] // 2
    per = CAP * HOMES
    pairs = part.shape[2] // per
    around = {0: [], 1: []}
    far = (4, 3, 5, 2, 6, 1, 7)

    def swap(m, g, k, t):
        return send(g.at[t, 1 - c], half_in.at[m, t], csend.at[m, k], crecv.at[m, k], other)

    def pass_on(m, g, copy, d, t):
        copy.wait()
        acc = g[t, c] + half_in[m, t]
        if d == 0:
            sums[m] = acc
            return
        narrow[m, t] = acc.astype(jnp.bfloat16)
        around[m].append(
            send(narrow.at[m, t], z_in.at[m, d - 1], zsend.at[m, d - 1], zrecv.at[m, d - 1], {"z": t})
        )

    order = [(d, step(ids, "z", d)) for d in far + (0,)]
    swaps = [swap(0, dec, k, t) for k, (d, t) in enumerate(order)]

    def beside():
        for copy, (d, t) in zip(swaps, order):
            pass_on(0, dec, copy, d, t)

    def middle(h, acc):
        at = pl.ds(h * half, half)
        codes[y, x, at] = (acc * slopes[at, :]).astype(jnp.bfloat16)

    finish(reduce_share(ids, part, codes, first, second, total, ssem, rsem, middle, beside))

    def make(t, h):
        q = 2 * t + h

        @pl.loop(0, pairs, unroll=True)
        def _(j):
            own = pl.ds(pl.multiple_of(j * per, per), per)
            code = codes[q // 4, lax.rem(q, 4), own, :]
            at = pl.ds(pl.multiple_of((q * pairs + j) * 2 * per, 2 * per), 2 * per)
            lanes = pl.ds(pl.multiple_of(j * LANES, LANES), LANES)
            enc[t, h, lanes, :] = dot(split_pair(code), rows[at, :], 0, 0)

    held = None
    for k, (d, t) in enumerate(order):
        make(t, 1 - c)
        copy = swap(1, enc, k, t)
        make(t, c)
        if held is not None:
            pass_on(1, enc, *held)
        held = (copy, d, t)
    pass_on(1, enc, *held)

    lat = dec_out.shape[0] // 2
    owner_c = x // 2
    lanes = pl.ds(pl.multiple_of(lax.rem(x, 2) * LANES, LANES), LANES)
    at = pl.ds(pl.multiple_of(c * lat, lat), lat)
    homes = []
    for m, out in ((0, dec_out), (1, enc_out)):
        finish(around[m])
        sums[m] += sum(z_in[m, d].astype(jnp.float32) for d in range(nz - 1))
        for t in range(4):
            src, dst = sums.at[m, pl.ds(t * lat, lat)], out.at[at, lanes]
            own = (t == x) & (owner_c == c)
            sem = hrecv.at[m, c, lax.rem(x, 2)]
            copy = pltpu.make_async_remote_copy(
                src_ref=src, dst_ref=dst, send_sem=hsend.at[m, t], recv_sem=sem,
                device_id={"x": t, "c": owner_c}, device_id_type=MESH,
            )
            keep = pltpu.make_async_copy(src, dst, sem)

            @pl.when(own)
            def _():
                keep.start()

            @pl.when(jnp.logical_not(own))
            def _():
                copy.start()

            homes.append((own, copy))
    for m, out in ((0, dec_out), (1, enc_out)):
        for h in range(2):
            for i in range(2):
                dst = out.at[pl.ds(h * lat, lat), pl.ds(i * LANES, LANES)]
                pltpu.make_async_copy(dst, dst, hrecv.at[m, h, i]).wait()
    for own, copy in homes:
        @pl.when(jnp.logical_not(own))
        def _():
            copy.wait_send()


def talk(kernel, outs, scratch, cid, *args):
    whole = pl.BlockSpec(memory_space=pltpu.VMEM)
    return pl.pallas_call(
        kernel,
        out_shape=[jax.ShapeDtypeStruct(s, t) for s, t in outs],
        in_specs=[whole] * len(args),
        out_specs=[whole] * len(outs),
        scratch_shapes=scratch,
        compiler_params=pltpu.CompilerParams(
            collective_id=cid, has_side_effects=True, vmem_limit_bytes=VMEM
        ),
        name=kernel.__name__,
    )(*args)


def sems(*shape):
    return pltpu.SemaphoreType.DMA(shape)


def local(
    tokens,
    block_ids,
    enc_bias,
    enc_master,
    dec_master,
    enc_first,
    enc_second,
    dec_first,
    dec_second,
):
    nz, nx = lax.axis_size("z"), lax.axis_size("x")
    ny, nc = lax.axis_size("y"), lax.axis_size("c")
    tok, width = tokens.shape
    lat, part = dec_master.shape
    blocks = lat // BLOCK * nz * nx
    half = lat // nc
    me = lax.axis_index("y") * nx + lax.axis_index("x")

    per_half = half // BLOCK
    local_b = block_ids % (nc * per_half)
    shard = block_ids // (nc * per_half)
    place = (
        ((shard // nx) * nc + local_b // per_half) * nx + shard % nx
    ) * per_half + local_b % per_half
    nums = jnp.arange(blocks, dtype=jnp.int32)[:, None]
    named = [nums == place[:, k][None, :] for k in range(2)]
    count = jnp.cumsum((named[0] | named[1]).astype(jnp.int32), axis=1) - 1
    rank = jnp.stack([jnp.sum(jnp.where(n, count, 0), axis=0) for n in named])
    pos = jnp.pad(rank * blocks + place.T, ((0, 6), (0, 0)))

    bf, f32 = jnp.bfloat16, jnp.float32
    per = CAP * HOMES
    rows_own = blocks // 2 // HOMES * per
    slices = tokens.reshape(tok, HOMES, LANES).transpose(1, 0, 2)
    own_w = nx * half
    slices, pos, enc, dec_own, bias = talk(
        spread_kernel,
        [
            ((HOMES, tok, LANES), bf),
            ((HOMES, 8, tok), jnp.int32),
            ((nz, nc, own_w, LANES), bf),
            ((own_w, LANES), bf),
            ((nz, nx, lat // LANES, LANES), f32),
        ],
        [sems(15), sems(15), sems(15), sems(15), sems(2, 2, 2), sems(2, 4), sems(2, 4), sems(2, 4),
         sems(8), sems(8), sems(3), sems(3), sems(3), sems(7), sems(7)],
        1,
        slices,
        pos,
        enc_master.astype(bf).T,
        dec_master.astype(bf),
        enc_bias.reshape(-1, LANES),
    )
    slices = slices.reshape(HOMES * tok, LANES)
    enc = enc.reshape(-1, LANES)
    bias = bias.reshape(nz, nx, nc, half).transpose(0, 2, 1, 3).reshape(HOMES, -1, 1, LANES)
    bias = lax.dynamic_index_in_dim(bias, me, 0, keepdims=False)
    bias = jnp.broadcast_to(bias, (bias.shape[0], per, LANES)).reshape(rows_own, LANES)

    codes = (blocks // 2 * per, LANES)
    grid4 = (ny, nx, rows_own, LANES)
    held = [pltpu.VMEM((blocks * per, LANES), f32)]
    stages = [
        pltpu.VMEM((2, 3, 4, rows_own // 2, LANES), bf),
        pltpu.VMEM((2, 3, rows_own // 2, LANES), f32),
        pltpu.VMEM((2, 4, rows_own // 2, LANES), f32),
        sems(4, 2, 3),
        sems(4, 2, 3),
    ]
    pre, rows = call(encode_kernel, [(codes, bf), ((blocks * per, LANES), bf)], held, "encode", slices, pos, enc)
    coded, slopes, dec = talk(
        code_kernel,
        [(grid4, bf), ((rows_own, LANES), f32), ((nz, nc, own_w, LANES), bf)],
        stages + [sems(7), sems(7), pltpu.SemaphoreType.DMA, pltpu.SemaphoreType.DMA, pltpu.SemaphoreType.DMA],
        2,
        pre.reshape(grid4),
        bias,
        dec_own,
    )
    cgrad, dgrad = call(
        decode_kernel,
        [(codes, bf), ((blocks * BLOCK, LANES), f32)],
        held,
        "decode",
        coded.reshape(codes),
        dec.reshape(-1, LANES),
        slices,
        pos,
    )
    whole = (nz, nc, own_w, LANES)
    enc_share, dec_share = talk(
        tail_kernel,
        [((lat, part), f32), ((lat, part), f32)],
        [pltpu.VMEM(grid4, bf)]
        + stages
        + [
            pltpu.VMEM(whole, f32),
            pltpu.VMEM((2, nz, own_w, LANES), f32),
            pltpu.VMEM((2, nz, own_w, LANES), bf),
            pltpu.VMEM((2, nz - 1, own_w, LANES), bf),
            pltpu.VMEM((2, own_w, LANES), f32),
            sems(2, 8), sems(2, 8), sems(2, 7), sems(2, 7), sems(2, 4), sems(2, 2, 2),
        ],
        3,
        cgrad.reshape(grid4),
        slopes,
        dgrad.reshape(whole),
        rows,
    )
    enc_share = enc_share.T
    enc_new, enc_first_new, enc_second_new = adam(enc_master, enc_share, enc_first, enc_second)
    dec_new, dec_first_new, dec_second_new = adam(dec_master, dec_share, dec_first, dec_second)
    return (enc_new, dec_new, enc_first_new, enc_second_new, dec_first_new, dec_second_new)


def solution(mesh):
    grid = Mesh(mesh.devices.reshape(8, 4, 4, 2), ("z", "x", "y", "c"))
    lat, rep = ("z", "x"), REP
    tok = P(rep + lat, None)
    enc, dec = P(rep, lat), P(lat, rep)
    return jax.shard_map(
        local,
        mesh=grid,
        in_specs=(tok, tok, P(lat), enc, dec, enc, enc, dec, dec),
        out_specs=(enc, dec, enc, enc, dec, dec),
        check_vma=False,
    )
```

```python
import functools

import jax
import jax.numpy as jnp
from jax import lax
from jax.experimental import pallas as pl
from jax.experimental.pallas import tpu as pltpu
from jax.sharding import Mesh, PartitionSpec as P

BLOCK = 64
CAP = 5
LANES = 128
HOMES = 16
VMEM = 62 * 2**20

learn_rate = 0.001
adam_eps = 1e-08
first_fix = 1.0 - 0.9**10
second_fix = 1.0 - 0.95**10

REP = ("y", "c")
CHIPS = ("y", "x")


def adam(master, gradient, first, second):
    first_new = 0.9 * first + 0.1 * gradient
    second_new = 0.95 * second + 0.05 * gradient * gradient
    update = first_new / first_fix / (jnp.sqrt(second_new / second_fix) + adam_eps)
    return (master - learn_rate * update, first_new, second_new)


def dot(a, b, ca, cb):
    return lax.dot_general(a, b, (((ca,), (cb,)), ((), ())), preferred_element_type=jnp.float32)


def low_lanes(shape):
    return lax.broadcasted_iota(jnp.int32, shape, 1) < BLOCK


def split_pair(pair):
    low = low_lanes(pair.shape)
    zero = jnp.zeros_like(pair)
    return jnp.concatenate([jnp.where(low, pair, zero), jnp.where(low, zero, pair)], axis=0)


def join_pair(both):
    half = both.shape[0] // 2
    return jnp.where(low_lanes((half, LANES)), both[:half], both[half:])


def slot_onehot(pos_ref, home, slot, blocks, tok):
    rows = (lax.broadcasted_iota(jnp.int32, (blocks, tok), 0) + slot * blocks).astype(jnp.int16)
    first = pos_ref[home, 0:1, :].astype(jnp.int16)
    second = pos_ref[home, 1:2, :].astype(jnp.int16)
    one, zero = jnp.ones((), jnp.bfloat16), jnp.zeros((), jnp.bfloat16)
    return jnp.where((rows == first) | (rows == second), one, zero)


MESH = pl.DeviceIdType.MESH


def axis_ids():
    return {a: lax.axis_index(a) for a in ("z", "x", "y", "c")}


def step(ids, axis, d):
    n = lax.axis_size(axis)
    return lax.rem(ids[axis] + (d + n), n)


def meet(peers):
    barrier = pltpu.get_barrier_semaphore()
    for peer in peers:
        pl.semaphore_signal(barrier, inc=1, device_id=peer, device_id_type=MESH)
    pl.semaphore_wait(barrier, len(peers))


def send(src, dst, ssem, rsem, peer):
    copy = pltpu.make_async_remote_copy(
        src_ref=src, dst_ref=dst, send_sem=ssem, recv_sem=rsem, device_id=peer, device_id_type=MESH
    )
    copy.start()
    return copy


def finish(copies):
    for copy in copies:
        copy.wait()


def ring_peers(ids, axis):
    return [{axis: step(ids, axis, d)} for d in range(1, lax.axis_size(axis))]


def reduce_share(ids, part, out, first, second, total, ssem, rsem, produce, middle, hooks):
    x, y = ids["x"], ids["y"]
    half = part.shape[2] // 2
    top, low = pl.ds(0, half), pl.ds(half, half)

    def stage(k, pairs, before=None):
        copies = []
        for d in (1, 3, 2):
            for h in range(2):
                if before is not None:
                    before(h, d)
                src, dst, peer = pairs(h, d)
                copies.append(send(src, dst, ssem.at[k, h, d - 1], rsem.at[k, h, d - 1], peer))
        return copies

    def one(h, d):
        if h == 0:
            t = step(ids, "x", d)
            return part.at[:, t, top], first.at[0, d - 1], {"x": t}
        t = step(ids, "y", d)
        return part.at[t, :, low], first.at[1, d - 1], {"y": t}

    copies = stage(0, one, produce)
    produce(0, 0)
    produce(1, 0)
    hooks[0]()
    finish(copies)
    hooks[1]()
    for k in range(4):
        for h, own in ((0, part.at[k, x, top]), (1, part.at[y, k, low])):
            acc = own[...].astype(jnp.float32)
            for d in range(3):
                acc += first[h, d, k].astype(jnp.float32)
            total[h, k] = acc

    def two(h, d):
        axis = "y" if h == 0 else "x"
        t = step(ids, axis, d)
        return total.at[h, t], second.at[h, d - 1], {axis: t}

    copies = stage(1, two)
    hooks[2]()
    finish(copies)
    for h, mine in ((0, y), (1, x)):
        acc = total[h, mine]
        for d in range(3):
            acc += second[h, d]
        middle(h, acc)

    def three(h, d):
        axis, rows = ("y", top) if h == 0 else ("x", low)
        return out.at[y, x, rows], out.at[y, x, rows], {axis: step(ids, axis, d)}

    copies = stage(2, three)
    hooks[3]()
    finish(copies)

    def four(h, d):
        if h == 0:
            return out.at[:, x, top], out.at[:, x, top], {"x": step(ids, "x", d)}
        return out.at[y, :, low], out.at[y, :, low], {"y": step(ids, "y", d)}

    copies = stage(3, four)
    hooks[4]()
    finish(copies)


def gelu_parts(v):
    a, b = 0.7978845608028654, 0.044715
    t = jnp.tanh(a * (v + b * (v * v * v)))
    value = 0.5 * v * (1.0 + t)
    slope = 0.5 * (1.0 + t) + 0.5 * v * (1.0 - t * t) * (a * (1.0 + 3.0 * b * (v * v)))
    return value, slope


class ZRing:
    def __init__(self, ids, buf, rsend, rrecv, csend, crecv):
        self.ids, self.buf, self.c = ids, buf, ids["c"]
        self.sems, self.core = (rsend, rrecv), (csend, crecv)
        self.half = buf.shape[2] // 2
        self.sent, self.over = {}, []

    def launch(self, k, s):
        for way, sign in ((0, 1), (1, -1)):
            if k < 3 or s == way:
                zz = step(self.ids, "z", -sign * k)
                piece = self.buf.at[zz, self.c, pl.ds(s * self.half, self.half)]
                sems = [sem.at[way, k, s] for sem in self.sems]
                self.sent[way, k, s] = send(piece, piece, *sems, {"z": step(self.ids, "z", sign)})

    def share(self, zz):
        n = len(self.over)
        block = self.buf.at[zz, self.c]
        sems = [sem.at[n] for sem in self.core]
        self.over.append(send(block, block, *sems, {"c": 1 - self.c}))

    def begin(self):
        for s in range(2):
            self.launch(0, s)
        self.share(self.ids["z"])

    def arrive(self, k):
        for s in range(2):
            for way in range(2):
                if k < 4 or s == way:
                    self.sent[way, k - 1, s].wait_recv()
            if k < 4:
                self.launch(k, s)
        self.share(step(self.ids, "z", -k))
        if k < 4:
            self.share(step(self.ids, "z", k))

    def end(self):
        for copy in self.sent.values():
            copy.wait_send()
        finish(self.over)


def swap_homes(ids, items, ssem, rsem):
    started = []
    for n, r, src, dst, tx, tc in items:
        own = (tx == ids["x"]) & (tc == ids["c"])
        copy = pltpu.make_async_remote_copy(
            src_ref=src, dst_ref=dst, send_sem=ssem.at[n], recv_sem=rsem.at[r],
            device_id={"x": tx, "c": tc}, device_id_type=MESH,
        )
        keep = pltpu.make_async_copy(src, dst, rsem.at[r])

        @pl.when(own)
        def _():
            keep.start()

        @pl.when(jnp.logical_not(own))
        def _():
            copy.start()

        started.append((own, copy))
    return started


def sent_homes(started):
    for own, copy in started:
        @pl.when(jnp.logical_not(own))
        def _():
            copy.wait_send()


def landed(dst, sem):
    pltpu.make_async_copy(dst, dst, sem).wait()


PLANE = (
    (1, 0), (0, 1), (3, 0), (0, 3), (1, 1), (3, 3), (1, 3), (3, 1),
    (2, 0), (0, 2), (1, 2), (2, 1), (3, 2), (2, 3), (2, 2),
)
FAR = (4, 3, 5, 2, 6, 1, 7, 0)


def train_kernel(names, *refs):
    tokens, place, enc, dec, bias, enc_out, dec_out = refs[:7]
    v = dict(zip(names, refs[7:]))
    ids = axis_ids()
    x, y, z, c = ids["x"], ids["y"], ids["z"], ids["c"]
    me = y * 4 + x
    other = {"c": 1 - c}
    per = CAP * HOMES
    held, rows, part, codes, pgrad = v["held"], v["rows"], v["part"], v["codes"], v["pgrad"]
    tok_all, pos_all, enc_all, dec_all = v["tok_all"], v["pos_all"], v["enc_all"], v["dec_all"]
    slopes, bias_all = v["slopes"], v["bias_all"]
    tok = tok_all.shape[1]
    pairs = part.shape[2] // per
    blocks = HOMES * pairs * 2
    lat = dec.shape[0] // 2
    bf, f32 = jnp.bfloat16, jnp.float32

    peers = [{"y": step(ids, "y", a), "x": step(ids, "x", b)} for a, b in PLANE]
    crossed = [{"x": step(ids, "x", d), "c": 1 - c} for d in range(4)]
    meet(peers + crossed + ring_peers(ids, "z"))

    swaps = []
    for m in range(2):
        for i in range(2):
            for h in range(2):
                at = pl.ds(pl.multiple_of(x * lat, lat), lat)
                if m == 0:
                    src = enc.at[pl.ds(i * LANES, LANES), pl.ds(h * lat, lat)]
                    dst = enc_all.at[z, h, :, at]
                else:
                    src = dec.at[pl.ds(h * lat, lat), pl.ds(i * LANES, LANES)]
                    dst = dec_all.at[z, h, at]
                swaps.append(((m, i, h), (m, x), src, dst, 2 * c + i, h))
    swaps = swap_homes(ids, swaps, _At(v["wsend"]), _At(v["wrecv"]))
    bias_x = [
        send(bias, bias_all.at[z, x], v["bsend"].at[d - 1], v["brecv"].at[d - 1], {"x": step(ids, "x", d)})
        for d in range(1, 4)
    ]
    keep = [
        pltpu.make_async_copy(bias, bias_all.at[z, x], v["lsem"].at[0]),
        pltpu.make_async_copy(
            tokens.at[:, pl.ds(pl.multiple_of(me * LANES, LANES), LANES)], tok_all.at[me], v["lsem"].at[1]
        ),
    ]
    for copy in keep:
        copy.start()
    got = []
    for n, (a, b) in enumerate(PLANE):
        t = step(ids, "y", a) * 4 + step(ids, "x", b)
        src = tokens.at[:, pl.ds(pl.multiple_of(t * LANES, LANES), LANES)]
        got.append(send(src, tok_all.at[me], v["tsend"].at[n], v["trecv"].at[n], peers[n]))

    numbers = lax.broadcasted_iota(jnp.int32, (blocks, tok), 0)
    named = [numbers == place[k : k + 1, :] for k in range(2)]
    one, zero = jnp.ones((), f32), jnp.zeros((), f32)
    either = jnp.where(named[0] | named[1], one, zero).astype(bf)
    before = lax.broadcasted_iota(jnp.int32, (tok, tok), 0) < lax.broadcasted_iota(jnp.int32, (tok, tok), 1)
    count = dot(either, jnp.where(before, one, zero).astype(bf), 1, 0)
    pos_all[me] = jnp.zeros(pos_all.shape[1:], jnp.int32)
    for k in range(2):
        rank = jnp.sum(jnp.where(named[k], count, zero), axis=0, keepdims=True).astype(jnp.int32)
        pos_all[me, k : k + 1, :] = rank * blocks + place[k : k + 1, :]
    got += [
        send(pos_all.at[me], pos_all.at[me], v["psend"].at[n], v["precv"].at[n], peers[n]) for n in range(15)
    ]

    ring = ZRing(ids, enc_all, v["ersend"], v["errecv"], v["ecsend"], v["ecrecv"])
    for src in range(4):
        landed(enc_all.at[z, c, :, pl.ds(src * lat, lat)], v["wrecv"].at[0, src])
    ring.begin()
    finish(bias_x)
    keep[0].wait()
    bias_z = [
        send(bias_all.at[z], bias_all.at[z], v["bzsend"].at[d - 1], v["bzrecv"].at[d - 1], {"z": step(ids, "z", d)})
        for d in range(1, 8)
    ]
    ring.arrive(1)
    ring.arrive(2)
    finish(got)
    keep[1].wait()

    def gather(homes):
        @pl.loop(*homes)
        def _(home):
            mine = tok_all[home]
            for slot in range(CAP):
                picked = dot(slot_onehot(pos_all, home, slot, blocks, tok), mine, 1, 0)
                held[pl.ds(slot * HOMES + home, blocks, per), :] = picked

    gather((0, 8))
    ring.arrive(3)
    gather((8, 16))
    ring.arrive(4)
    around = ZRing(ids, dec_all, v["drsend"], v["drrecv"], v["dcsend"], v["dcrecv"])
    for src in range(4):
        landed(dec_all.at[z, c, pl.ds(src * lat, lat)], v["wrecv"].at[1, src])
    around.begin()
    finish(bias_z)
    ring.end()

    def pair_rows(q, j):
        return pl.ds(pl.multiple_of((q * pairs + j) * 2 * per, 2 * per), 2 * per)

    def code_rows(j):
        return pl.ds(pl.multiple_of(j * per, per), per)

    def weight_rows(j):
        return pl.ds(pl.multiple_of(j * LANES, LANES), LANES)

    def own_pairs(ref, q, j):
        return ref.at[lax.div(q, 4), lax.rem(q, 4), code_rows(j), :]

    def groups(body):
        def produce(h, d):
            t = step(ids, "xy"[h], d)

            @pl.loop(0, 4)
            def _(k):
                q = 4 * k + t if h == 0 else 4 * t + k
                for j in range(pairs // 2):
                    body(q, h * (pairs // 2) + j)

        return produce

    def encode(q, j):
        mine = held[pair_rows(q, j), :].astype(bf)
        rows[pair_rows(q, j), :] = mine
        weight = enc_all[lax.div(q, 2), lax.rem(q, 2), :, weight_rows(j)]
        own_pairs(part, q, j)[...] = join_pair(dot(mine, weight, 1, 0)).astype(bf)

    def activate(h, acc):
        for k in range(pairs // 2):
            j = h * (pairs // 2) + k
            shift = bias_all[lax.div(me, 2), j // 2, pl.ds(2 * lax.rem(me, 2) + j % 2, 1), :]
            value, slope = gelu_parts(acc[k * per : (k + 1) * per] + shift)
            codes[y, x, j * per : (j + 1) * per] = value.astype(bf)
            slopes[j * per : (j + 1) * per, :] = slope

    stages = [v[k] for k in ("first", "second", "total")]
    nothing = lambda: None
    reduce_share(
        ids, part, codes, *stages, v["ssend"].at[0], v["srecv"].at[0], groups(encode), activate,
        [lambda: around.arrive(1), lambda: around.arrive(2), lambda: around.arrive(3), lambda: around.arrive(4), nothing],
    )
    around.end()

    @pl.loop(0, HOMES)
    def _(q):
        for j in range(pairs):
            weight = dec_all[lax.div(q, 2), lax.rem(q, 2), weight_rows(j), :]
            held[pair_rows(q, j), :] = dot(split_pair(own_pairs(codes, q, j)[...]), weight, 1, 0)

    @pl.loop(0, HOMES)
    def _(home):
        hots = [slot_onehot(pos_all, home, slot, blocks, tok) for slot in range(CAP)]
        rebuilt = jnp.zeros((tok, LANES), f32)
        for slot in range(CAP):
            some = held[pl.ds(slot * HOMES + home, blocks, per), :].astype(bf)
            rebuilt += dot(hots[slot], some, 0, 0)
        err = (rebuilt - tok_all[home].astype(f32)).astype(bf)
        for slot in range(CAP):
            held[pl.ds(slot * HOMES + home, blocks, per), :] = dot(hots[slot], err, 1, 0)

    def code_grad(q, j):
        err = held[pair_rows(q, j), :].astype(bf)
        weight = dec_all[lax.div(q, 2), lax.rem(q, 2), weight_rows(j), :]
        own_pairs(part, q, j)[...] = join_pair(dot(err, weight, 1, 1)).astype(bf)

    def dec_grad(q, j):
        err = held[pair_rows(q, j), :].astype(bf)
        return dot(split_pair(own_pairs(codes, q, j)[...]), err, 0, 0)

    def enc_grad(q, j):
        return dot(rows[pair_rows(q, j), :], split_pair(own_pairs(pgrad, q, j)[...]), 0, 0)

    def collect(m, grad, name):
        out, half_in, narrow, z_in, sums = (v[name + k] for k in ("out", "half", "narrow", "z_in", "sums"))

        def slot(ref, j, *lead):
            return ref.at[(*lead, slice(None), weight_rows(j))] if m else ref.at[(*lead, weight_rows(j))]

        sent = []

        def pass_on(copy, d, t):
            copy.wait()
            for j in range(pairs):
                acc = grad(2 * t + c, j) + slot(half_in, j, t)[...]
                if d == 0:
                    slot(sums, j)[...] = acc
                else:
                    slot(narrow, j, t)[...] = acc.astype(bf)
            if d:
                sems = [v[k].at[m, d - 1] for k in ("zsend", "zrecv")]
                sent.append(send(narrow.at[t], z_in.at[d - 1], *sems, {"z": t}))

        last = None
        for k, d in enumerate(FAR):
            t = step(ids, "z", d)
            for j in range(pairs):
                slot(out, j, k % 2)[...] = grad(2 * t + 1 - c, j)
            copy = send(out.at[k % 2], half_in.at[t], v["csend"].at[m, k], v["crecv"].at[m, k], other)
            if last is not None:
                pass_on(*last)
            last = (copy, d, t)
        pass_on(*last)
        return sent

    sent = []

    def multiply(h, acc):
        at = pl.ds(h * acc.shape[0], acc.shape[0])
        pgrad[y, x, at] = (acc * slopes[at, :]).astype(bf)

    reduce_share(
        ids, part, pgrad, *stages, v["ssend"].at[1], v["srecv"].at[1], groups(code_grad), multiply,
        [lambda: sent.extend(collect(0, dec_grad, "d_")), nothing, nothing, nothing, nothing],
    )
    dec_sent = list(sent)
    enc_sent = collect(1, enc_grad, "e_")

    homes = []
    for m, name, around_z, dst in ((0, "d_", dec_sent, dec_out), (1, "e_", enc_sent, enc_out)):
        finish(around_z)
        sums, z_in = v[name + "sums"], v[name + "z_in"]
        sums[...] += sum(z_in[d].astype(f32) for d in range(z_in.shape[0]))
        at = pl.ds(pl.multiple_of(c * lat, lat), lat)
        lanes = pl.ds(pl.multiple_of(lax.rem(x, 2) * LANES, LANES), LANES)
        items = []
        for t in range(4):
            piece = pl.ds(t * lat, lat)
            if m == 0:
                src, to = sums.at[piece], dst.at[at, lanes]
            else:
                src, to = sums.at[:, piece], dst.at[lanes, at]
            items.append(((m, t), (m, c, lax.rem(x, 2)), src, to, t, lax.div(x, 2)))
        homes += swap_homes(ids, items, _At(v["hsend"]), _At(v["hrecv"]))
    for m, dst in ((0, dec_out), (1, enc_out)):
        for h in range(2):
            for i in range(2):
                at, lanes = pl.ds(h * lat, lat), pl.ds(i * LANES, LANES)
                landed(dst.at[at, lanes] if m == 0 else dst.at[lanes, at], v["hrecv"].at[m, h, i])
    sent_homes(swaps)
    sent_homes(homes)


class _At:
    def __init__(self, ref):
        self.ref = ref

    @property
    def at(self):
        return self

    def __getitem__(self, index):
        return self.ref.at[index]


def sems(*shape):
    return pltpu.SemaphoreType.DMA(shape)


def local(
    tokens,
    block_ids,
    enc_bias,
    enc_master,
    dec_master,
    enc_first,
    enc_second,
    dec_first,
    dec_second,
):
    nz, nx = lax.axis_size("z"), lax.axis_size("x")
    ny, nc = lax.axis_size("y"), lax.axis_size("c")
    tok, width = tokens.shape
    lat, part = dec_master.shape
    blocks = lat // BLOCK * nz * nx
    half = lat // nc
    bf, f32 = jnp.bfloat16, jnp.float32

    per_half = half // BLOCK
    local_b = block_ids % (nc * per_half)
    shard = block_ids // (nc * per_half)
    place = (
        ((shard // nx) * nc + local_b // per_half) * nx + shard % nx
    ) * per_half + local_b % per_half

    per = CAP * HOMES
    rows_own = blocks // 2 // HOMES * per
    own_w = nx * half
    grid4 = (ny, nx, rows_own, LANES)
    w_enc, w_dec = (LANES, own_w), (own_w, LANES)
    scratch = {
        "held": pltpu.VMEM((blocks * per, LANES), f32),
        "rows": pltpu.VMEM((blocks * per, LANES), bf),
        "part": pltpu.VMEM(grid4, bf),
        "codes": pltpu.VMEM(grid4, bf),
        "pgrad": pltpu.VMEM(grid4, bf),
        "tok_all": pltpu.VMEM((HOMES, tok, LANES), bf),
        "pos_all": pltpu.VMEM((HOMES, 8, tok), jnp.int32),
        "enc_all": pltpu.VMEM((nz, nc) + w_enc, bf),
        "dec_all": pltpu.VMEM((nz, nc) + w_dec, bf),
        "slopes": pltpu.VMEM((rows_own, LANES), f32),
        "bias_all": pltpu.VMEM((nz, nx, lat // LANES, LANES), f32),
        "first": pltpu.VMEM((2, 3, 4, rows_own // 2, LANES), bf),
        "second": pltpu.VMEM((2, 3, rows_own // 2, LANES), f32),
        "total": pltpu.VMEM((2, 4, rows_own // 2, LANES), f32),
    }
    for name, shape in (("d_", w_dec), ("e_", w_enc)):
        scratch[name + "out"] = pltpu.VMEM((2,) + shape, f32)
        scratch[name + "half"] = pltpu.VMEM((nz,) + shape, f32)
        scratch[name + "narrow"] = pltpu.VMEM((nz,) + shape, bf)
        scratch[name + "z_in"] = pltpu.VMEM((nz - 1,) + shape, bf)
        scratch[name + "sums"] = pltpu.VMEM(shape, f32)
    for name, shape in (
        ("w", (2, 2, 2)), ("b", (3,)), ("t", (15,)), ("p", (15,)), ("er", (2, 4, 2)), ("ec", (8,)),
        ("dr", (2, 4, 2)), ("dc", (8,)), ("bz", (7,)), ("s", (2, 4, 2, 3)), ("c", (2, 8)), ("z", (2, 7)),
    ):
        scratch[name + "send"] = sems(*shape)
        scratch[name + "recv"] = sems(*((2, 4) if name == "w" else shape))
    scratch.update(lsem=sems(2), hsend=sems(2, 4), hrecv=sems(2, 2, 2))

    vmem = pl.BlockSpec(memory_space=pltpu.VMEM)
    enc_share, dec_share = pl.pallas_call(
        functools.partial(train_kernel, tuple(scratch)),
        out_shape=[jax.ShapeDtypeStruct((part, lat), f32), jax.ShapeDtypeStruct((lat, part), f32)],
        in_specs=[pl.BlockSpec(memory_space=pl.ANY)] + [vmem] * 4,
        out_specs=[vmem] * 2,
        scratch_shapes=list(scratch.values()),
        compiler_params=pltpu.CompilerParams(
            collective_id=1, has_side_effects=True, vmem_limit_bytes=VMEM
        ),
        name="train",
    )(tokens, place.T, enc_master.astype(bf), dec_master.astype(bf), enc_bias.reshape(-1, LANES))
    enc_new, enc_first_new, enc_second_new = adam(enc_master, enc_share, enc_first, enc_second)
    dec_new, dec_first_new, dec_second_new = adam(dec_master, dec_share, dec_first, dec_second)
    return (enc_new, dec_new, enc_first_new, enc_second_new, dec_first_new, dec_second_new)


def solution(mesh):
    grid = Mesh(mesh.devices.reshape(8, 4, 4, 2), ("z", "x", "y", "c"))
    lat, rep = ("z", "x"), REP
    tok = P(rep + lat, None)
    enc, dec = P(rep, lat), P(lat, rep)
    return jax.shard_map(
        local,
        mesh=grid,
        in_specs=(tok, tok, P(lat), enc, dec, enc, enc, dec, dec),
        out_specs=(enc, dec, enc, enc, dec, dec),
        check_vma=False,
    )
```

```python
import functools

import jax
import jax.numpy as jnp
from jax import lax
from jax.experimental import pallas as pl
from jax.experimental.pallas import tpu as pltpu
from jax.sharding import Mesh, PartitionSpec as P

BLOCK = 64
CAP = 5
LANES = 128
HOMES = 16
VMEM = 62 * 2**20

learn_rate = 0.001
adam_eps = 1e-08
first_fix = 1.0 - 0.9**10
second_fix = 1.0 - 0.95**10

REP = ("y", "c")
CHIPS = ("y", "x")


def adam(master, gradient, first, second):
    first_new = 0.9 * first + 0.1 * gradient
    second_new = 0.95 * second + 0.05 * gradient * gradient
    update = first_new / first_fix / (jnp.sqrt(second_new / second_fix) + adam_eps)
    return (master - learn_rate * update, first_new, second_new)


def dot(a, b, ca, cb):
    return lax.dot_general(a, b, (((ca,), (cb,)), ((), ())), preferred_element_type=jnp.float32)


def low_lanes(shape):
    return lax.broadcasted_iota(jnp.int32, shape, 1) < BLOCK


def split_pair(pair):
    low = low_lanes(pair.shape)
    zero = jnp.zeros_like(pair)
    return jnp.concatenate([jnp.where(low, pair, zero), jnp.where(low, zero, pair)], axis=0)


def join_pair(both):
    half = both.shape[0] // 2
    return jnp.where(low_lanes((half, LANES)), both[:half], both[half:])


def slot_onehot(pos_ref, home, slot, blocks, tok):
    rows = (lax.broadcasted_iota(jnp.int32, (blocks, tok), 0) + slot * blocks).astype(jnp.int16)
    first = pos_ref[home, 0:1, :].astype(jnp.int16)
    second = pos_ref[home, 1:2, :].astype(jnp.int16)
    one, zero = jnp.ones((), jnp.bfloat16), jnp.zeros((), jnp.bfloat16)
    return jnp.where((rows == first) | (rows == second), one, zero)


MESH = pl.DeviceIdType.MESH


def axis_ids():
    return {a: lax.axis_index(a) for a in ("z", "x", "y", "c")}


def step(ids, axis, d):
    n = lax.axis_size(axis)
    return lax.rem(ids[axis] + (d + n), n)


def meet(peers):
    barrier = pltpu.get_barrier_semaphore()
    for peer in peers:
        pl.semaphore_signal(barrier, inc=1, device_id=peer, device_id_type=MESH)
    pl.semaphore_wait(barrier, len(peers))


def send(src, dst, ssem, rsem, peer):
    copy = pltpu.make_async_remote_copy(
        src_ref=src, dst_ref=dst, send_sem=ssem, recv_sem=rsem, device_id=peer, device_id_type=MESH
    )
    copy.start()
    return copy


def finish(copies):
    for copy in copies:
        copy.wait()


def ring_peers(ids, axis):
    return [{axis: step(ids, axis, d)} for d in range(1, lax.axis_size(axis))]


def reduce_share(ids, part, out, first, second, total, ssem, rsem, produce, middle, hooks):
    x, y = ids["x"], ids["y"]
    half = part.shape[2] // 2
    top, low = pl.ds(0, half), pl.ds(half, half)

    def stage(k, h, pairs):
        copies = []
        for d in (1, 3, 2):
            src, dst, peer = pairs(h, d)
            copies.append(send(src, dst, ssem.at[k, h, d - 1], rsem.at[k, h, d - 1], peer))
        return copies

    def one(h, d):
        if h == 0:
            t = step(ids, "x", d)
            return part.at[:, t, top], first.at[0, d - 1], {"x": t}
        t = step(ids, "y", d)
        return part.at[t, :, low], first.at[1, d - 1], {"y": t}

    def two(h, d):
        axis = "y" if h == 0 else "x"
        t = step(ids, axis, d)
        return total.at[h, t], second.at[h, d - 1], {axis: t}

    def three(h, d):
        axis, rows = ("y", top) if h == 0 else ("x", low)
        return out.at[y, x, rows], out.at[y, x, rows], {axis: step(ids, axis, d)}

    def four(h, d):
        if h == 0:
            return out.at[:, x, top], out.at[:, x, top], {"x": step(ids, "x", d)}
        return out.at[y, :, low], out.at[y, :, low], {"y": step(ids, "y", d)}

    sent = [[], []]
    for d in (1, 3, 2):
        for h in range(2):
            produce(h, d)
            src, dst, peer = one(h, d)
            sent[h].append(send(src, dst, ssem.at[0, h, d - 1], rsem.at[0, h, d - 1], peer))
    produce(0, 0)
    produce(1, 0)
    hooks[0]()
    for h in range(2):
        finish(sent[h])
        for k in range(4):
            own = part.at[k, x, top] if h == 0 else part.at[y, k, low]
            acc = own[...].astype(jnp.float32)
            for d in range(3):
                acc += first[h, d, k].astype(jnp.float32)
            total[h, k] = acc
        sent[h] = stage(1, h, two)
    hooks[1]()
    for h, mine in ((0, y), (1, x)):
        finish(sent[h])
        acc = total[h, mine]
        for d in range(3):
            acc += second[h, d]
        middle(h, acc)
        sent[h] = stage(2, h, three)
    hooks[2]()
    for h in range(2):
        finish(sent[h])
        sent[h] = stage(3, h, four)
    hooks[3]()
    finish(sent[0] + sent[1])


def gelu_parts(v):
    a, b = 0.7978845608028654, 0.044715
    t = jnp.tanh(a * (v + b * (v * v * v)))
    value = 0.5 * v * (1.0 + t)
    slope = 0.5 * (1.0 + t) + 0.5 * v * (1.0 - t * t) * (a * (1.0 + 3.0 * b * (v * v)))
    return value, slope


class ZRing:
    def __init__(self, ids, buf, rsend, rrecv, csend, crecv):
        self.ids, self.buf, self.c = ids, buf, ids["c"]
        self.sems, self.core = (rsend, rrecv), (csend, crecv)
        self.half = buf.shape[2] // 2
        self.sent, self.over = {}, []

    def launch(self, k, s):
        for way, sign in ((0, 1), (1, -1)):
            if k < 3 or s == way:
                zz = step(self.ids, "z", -sign * k)
                piece = self.buf.at[zz, self.c, pl.ds(s * self.half, self.half)]
                sems = [sem.at[way, k, s] for sem in self.sems]
                self.sent[way, k, s] = send(piece, piece, *sems, {"z": step(self.ids, "z", sign)})

    def share(self, zz):
        n = len(self.over)
        block = self.buf.at[zz, self.c]
        sems = [sem.at[n] for sem in self.core]
        self.over.append(send(block, block, *sems, {"c": 1 - self.c}))

    def begin(self):
        for s in range(2):
            self.launch(0, s)
        self.share(self.ids["z"])

    def arrive(self, k):
        for s in range(2):
            for way in range(2):
                if k < 4 or s == way:
                    self.sent[way, k - 1, s].wait_recv()
            if k < 4:
                self.launch(k, s)
        self.share(step(self.ids, "z", -k))
        if k < 4:
            self.share(step(self.ids, "z", k))

    def end(self):
        for copy in self.sent.values():
            copy.wait_send()
        finish(self.over)


def swap_homes(ids, items, ssem, rsem):
    started = []
    for n, r, src, dst, tx, tc in items:
        own = (tx == ids["x"]) & (tc == ids["c"])
        copy = pltpu.make_async_remote_copy(
            src_ref=src, dst_ref=dst, send_sem=ssem.at[n], recv_sem=rsem.at[r],
            device_id={"x": tx, "c": tc}, device_id_type=MESH,
        )
        keep = pltpu.make_async_copy(src, dst, rsem.at[r])

        @pl.when(own)
        def _():
            keep.start()

        @pl.when(jnp.logical_not(own))
        def _():
            copy.start()

        started.append((own, copy))
    return started


def sent_homes(started):
    for own, copy in started:
        @pl.when(jnp.logical_not(own))
        def _():
            copy.wait_send()


def landed(dst, sem):
    pltpu.make_async_copy(dst, dst, sem).wait()


PLANE = (
    (1, 0), (0, 1), (3, 0), (0, 3), (1, 1), (3, 3), (1, 3), (3, 1),
    (2, 0), (0, 2), (1, 2), (2, 1), (3, 2), (2, 3), (2, 2),
)
FAR = (4, 3, 5, 2, 6, 1, 7, 0)


def train_kernel(names, *refs):
    tokens, place, enc, dec, bias, enc_out, dec_out = refs[:7]
    v = dict(zip(names, refs[7:]))
    ids = axis_ids()
    x, y, z, c = ids["x"], ids["y"], ids["z"], ids["c"]
    me = y * 4 + x
    other = {"c": 1 - c}
    per = CAP * HOMES
    held, rows, part, codes, pgrad = v["held"], v["rows"], v["part"], v["codes"], v["pgrad"]
    tok_all, pos_all, enc_all, dec_all = v["tok_all"], v["pos_all"], v["enc_all"], v["dec_all"]
    slopes, bias_all = v["slopes"], v["bias_all"]
    tok = tok_all.shape[1]
    pairs = part.shape[2] // per
    blocks = HOMES * pairs * 2
    lat = dec.shape[0] // 2
    bf, f32 = jnp.bfloat16, jnp.float32

    peers = [{"y": step(ids, "y", a), "x": step(ids, "x", b)} for a, b in PLANE]
    crossed = [{"x": step(ids, "x", d), "c": 1 - c} for d in range(4)]
    meet(peers + crossed + ring_peers(ids, "z"))

    swaps = []
    for m in range(2):
        for i in range(2):
            for h in range(2):
                at = pl.ds(pl.multiple_of(x * lat, lat), lat)
                if m == 0:
                    src = enc.at[pl.ds(i * LANES, LANES), pl.ds(h * lat, lat)]
                    dst = enc_all.at[z, h, :, at]
                else:
                    src = dec.at[pl.ds(h * lat, lat), pl.ds(i * LANES, LANES)]
                    dst = dec_all.at[z, h, at]
                swaps.append(((m, i, h), (m, x), src, dst, 2 * c + i, h))
    swaps = swap_homes(ids, swaps, _At(v["wsend"]), _At(v["wrecv"]))
    bias_x = [
        send(bias, bias_all.at[z, x], v["bsend"].at[d - 1], v["brecv"].at[d - 1], {"x": step(ids, "x", d)})
        for d in range(1, 4)
    ]
    keep = [
        pltpu.make_async_copy(bias, bias_all.at[z, x], v["lsem"].at[0]),
        pltpu.make_async_copy(
            tokens.at[:, pl.ds(pl.multiple_of(me * LANES, LANES), LANES)], tok_all.at[me], v["lsem"].at[1]
        ),
    ]
    for copy in keep:
        copy.start()
    got = []
    for n, (a, b) in enumerate(PLANE):
        t = step(ids, "y", a) * 4 + step(ids, "x", b)
        src = tokens.at[:, pl.ds(pl.multiple_of(t * LANES, LANES), LANES)]
        got.append(send(src, tok_all.at[me], v["tsend"].at[n], v["trecv"].at[n], peers[n]))

    numbers = lax.broadcasted_iota(jnp.int32, (blocks, tok), 0)
    named = [numbers == place[k : k + 1, :] for k in range(2)]
    one, zero = jnp.ones((), f32), jnp.zeros((), f32)
    either = jnp.where(named[0] | named[1], one, zero).astype(bf)
    before = lax.broadcasted_iota(jnp.int32, (tok, tok), 0) < lax.broadcasted_iota(jnp.int32, (tok, tok), 1)
    count = dot(either, jnp.where(before, one, zero).astype(bf), 1, 0)
    pos_all[me] = jnp.zeros(pos_all.shape[1:], jnp.int32)
    for k in range(2):
        rank = jnp.sum(jnp.where(named[k], count, zero), axis=0, keepdims=True).astype(jnp.int32)
        pos_all[me, k : k + 1, :] = rank * blocks + place[k : k + 1, :]
    got += [
        send(pos_all.at[me], pos_all.at[me], v["psend"].at[n], v["precv"].at[n], peers[n]) for n in range(15)
    ]

    ring = ZRing(ids, enc_all, v["ersend"], v["errecv"], v["ecsend"], v["ecrecv"])
    for src in range(4):
        landed(enc_all.at[z, c, :, pl.ds(src * lat, lat)], v["wrecv"].at[0, src])
    ring.begin()
    finish(bias_x)
    keep[0].wait()
    bias_z = [
        send(bias_all.at[z], bias_all.at[z], v["bzsend"].at[d - 1], v["bzrecv"].at[d - 1], {"z": step(ids, "z", d)})
        for d in range(1, 8)
    ]
    ring.arrive(1)
    ring.arrive(2)
    finish(got)
    keep[1].wait()

    def gather(homes):
        @pl.loop(*homes)
        def _(home):
            mine = tok_all[home]
            for slot in range(CAP):
                picked = dot(slot_onehot(pos_all, home, slot, blocks, tok), mine, 1, 0)
                held[pl.ds(slot * HOMES + home, blocks, per), :] = picked

    gather((0, 8))
    ring.arrive(3)
    gather((8, 16))
    ring.arrive(4)
    around = ZRing(ids, dec_all, v["drsend"], v["drrecv"], v["dcsend"], v["dcrecv"])
    for src in range(4):
        landed(dec_all.at[z, c, pl.ds(src * lat, lat)], v["wrecv"].at[1, src])
    around.begin()
    finish(bias_z)
    ring.end()

    def pair_rows(q, j):
        return pl.ds(pl.multiple_of((q * pairs + j) * 2 * per, 2 * per), 2 * per)

    def code_rows(j):
        return pl.ds(pl.multiple_of(j * per, per), per)

    def weight_rows(j):
        return pl.ds(pl.multiple_of(j * LANES, LANES), LANES)

    def own_pairs(ref, q, j):
        return ref.at[lax.div(q, 4), lax.rem(q, 4), code_rows(j), :]

    def groups(body):
        def produce(h, d):
            t = step(ids, "xy"[h], d)

            @pl.loop(0, 4)
            def _(k):
                q = 4 * k + t if h == 0 else 4 * t + k
                for j in range(pairs // 2):
                    body(q, h * (pairs // 2) + j)

        return produce

    def encode(q, j):
        mine = held[pair_rows(q, j), :].astype(bf)
        rows[pair_rows(q, j), :] = mine
        weight = enc_all[lax.div(q, 2), lax.rem(q, 2), :, weight_rows(j)]
        own_pairs(part, q, j)[...] = join_pair(dot(mine, weight, 1, 0)).astype(bf)

    def activate(h, acc):
        for k in range(pairs // 2):
            j = h * (pairs // 2) + k
            shift = bias_all[lax.div(me, 2), j // 2, pl.ds(2 * lax.rem(me, 2) + j % 2, 1), :]
            value, slope = gelu_parts(acc[k * per : (k + 1) * per] + shift)
            codes[y, x, j * per : (j + 1) * per] = value.astype(bf)
            slopes[j * per : (j + 1) * per, :] = slope

    stages = [v[k] for k in ("first", "second", "total")]
    reduce_share(
        ids, part, codes, *stages, v["ssend"].at[0], v["srecv"].at[0], groups(encode), activate,
        [lambda k=k: around.arrive(k) for k in range(1, 5)],
    )
    around.end()

    @pl.loop(0, HOMES)
    def _(q):
        for j in range(pairs):
            weight = dec_all[lax.div(q, 2), lax.rem(q, 2), weight_rows(j), :]
            held[pair_rows(q, j), :] = dot(split_pair(own_pairs(codes, q, j)[...]), weight, 1, 0)

    @pl.loop(0, HOMES, unroll=2)
    def _(home):
        hots = jnp.concatenate([slot_onehot(pos_all, home, slot, blocks, tok) for slot in range(CAP)], axis=0)
        at = [pl.ds(slot * HOMES + home, blocks, per) for slot in range(CAP)]
        some = jnp.concatenate([held[a, :].astype(bf) for a in at], axis=0)
        rebuilt = dot(some, hots, 0, 0)
        err = (rebuilt - tok_all[home].astype(f32).T).astype(bf)
        picked = dot(hots, err, 1, 1)
        for slot in range(CAP):
            held[at[slot], :] = picked[slot * blocks : (slot + 1) * blocks]

    def code_grad(q, j):
        err = held[pair_rows(q, j), :].astype(bf)
        weight = dec_all[lax.div(q, 2), lax.rem(q, 2), weight_rows(j), :]
        own_pairs(part, q, j)[...] = join_pair(dot(err, weight, 1, 1)).astype(bf)

    def dec_grad(q, j):
        err = held[pair_rows(q, j), :].astype(bf)
        return dot(split_pair(own_pairs(codes, q, j)[...]), err, 0, 0)

    def enc_grad(q, j):
        return dot(rows[pair_rows(q, j), :], split_pair(own_pairs(pgrad, q, j)[...]), 0, 0)

    def collect(m, grad, name):
        out, half_in, narrow, z_in, sums = (v[name + k] for k in ("out", "half", "narrow", "z_in", "sums"))

        def slot(ref, j, *lead):
            return ref.at[(*lead, slice(None), weight_rows(j))] if m else ref.at[(*lead, weight_rows(j))]

        sent, chain = [], {}

        def cut_rows(way):
            cut = z_in.shape[2] // 2
            return pl.ds(way * cut, cut)

        def ring_on(d, t):
            ways = (0, 1) if d == 4 else (0,) if 0 < d < 4 else (1,) if d else ()
            for way in ways:
                k = min(d, 8 - d)
                src, dst = narrow.at[t], z_in.at[way, k - 1]
                if k == 4:
                    src, dst = narrow.at[t, cut_rows(way)], z_in.at[way, 3, cut_rows(way)]
                sems = [v[n].at[way, k - 1] for n in ("grsend", "grrecv")]
                chain[way, k] = send(src, dst, *sems, {"z": step(ids, "z", 1 - 2 * way)})
                sent.append(chain[way, k])

        def pass_on(copy, d, t):
            copy.wait()
            way, k = (0, d) if d < 4 else (1, 8 - d)
            if m and d == 0:
                chain[0, 1].wait_recv()
                chain[1, 1].wait_recv()
            elif m and d != 4:
                chain[way, k + 1].wait_recv()
            for j in range(pairs):
                acc = grad(2 * t + c, j) + slot(half_in, j, t)[...]
                if m and d and d != 4:
                    came = slot(z_in, j, way, k)
                    if k == 3:
                        cut = acc.shape[0] // 2
                        lower, upper = acc[:cut], acc[cut:]
                        if way == 0:
                            lower += came[:cut].astype(f32)
                        else:
                            upper += came[cut:].astype(f32)
                        acc = jnp.concatenate([lower, upper], axis=0)
                    else:
                        acc += came[...].astype(f32)
                if m and d == 0:
                    acc += slot(z_in, j, 0, 0)[...].astype(f32) + slot(z_in, j, 1, 0)[...].astype(f32)
                if d == 0:
                    slot(sums, j)[...] = acc
                else:
                    slot(narrow, j, t)[...] = acc.astype(bf)
            if m:
                ring_on(d, t)
            elif d:
                sems = [v[k].at[m, d - 1] for k in ("zsend", "zrecv")]
                sent.append(send(narrow.at[t], z_in.at[d - 1], *sems, {"z": t}))

        last = None
        for k, d in enumerate(FAR):
            t = step(ids, "z", d)
            for j in range(pairs):
                slot(out, j, k % 2)[...] = grad(2 * t + 1 - c, j)
            copy = send(out.at[k % 2], half_in.at[t], v["csend"].at[m, k], v["crecv"].at[m, k], other)
            if last is not None:
                pass_on(*last)
            last = (copy, d, t)
        pass_on(*last)
        return sent

    sent = []

    def multiply(h, acc):
        at = pl.ds(h * acc.shape[0], acc.shape[0])
        pgrad[y, x, at] = (acc * slopes[at, :]).astype(bf)

    reduce_share(
        ids, part, pgrad, *stages, v["ssend"].at[1], v["srecv"].at[1], groups(code_grad), multiply,
        [lambda: sent.extend(collect(0, dec_grad, "d_"))] + [lambda: None] * 3,
    )
    dec_sent = list(sent)
    enc_sent = collect(1, enc_grad, "e_")

    homes = []
    for m, name, around_z, dst in ((0, "d_", dec_sent, dec_out), (1, "e_", enc_sent, enc_out)):
        sums, z_in = v[name + "sums"], v[name + "z_in"]
        if m == 0:
            finish(around_z)
            sums[...] += sum(z_in[d].astype(f32) for d in range(z_in.shape[0]))
        else:
            for copy in around_z:
                copy.wait_send()
        at = pl.ds(pl.multiple_of(c * lat, lat), lat)
        lanes = pl.ds(pl.multiple_of(lax.rem(x, 2) * LANES, LANES), LANES)
        items = []
        for t in range(4):
            piece = pl.ds(t * lat, lat)
            if m == 0:
                src, to = sums.at[piece], dst.at[at, lanes]
            else:
                src, to = sums.at[:, piece], dst.at[lanes, at]
            items.append(((m, t), (m, c, lax.rem(x, 2)), src, to, t, lax.div(x, 2)))
        homes += swap_homes(ids, items, _At(v["hsend"]), _At(v["hrecv"]))
    for m, dst in ((0, dec_out), (1, enc_out)):
        for h in range(2):
            for i in range(2):
                at, lanes = pl.ds(h * lat, lat), pl.ds(i * LANES, LANES)
                landed(dst.at[at, lanes] if m == 0 else dst.at[lanes, at], v["hrecv"].at[m, h, i])
    sent_homes(swaps)
    sent_homes(homes)


class _At:
    def __init__(self, ref):
        self.ref = ref

    @property
    def at(self):
        return self

    def __getitem__(self, index):
        return self.ref.at[index]


def sems(*shape):
    return pltpu.SemaphoreType.DMA(shape)


def local(
    tokens,
    block_ids,
    enc_bias,
    enc_master,
    dec_master,
    enc_first,
    enc_second,
    dec_first,
    dec_second,
):
    nz, nx = lax.axis_size("z"), lax.axis_size("x")
    ny, nc = lax.axis_size("y"), lax.axis_size("c")
    tok, width = tokens.shape
    lat, part = dec_master.shape
    blocks = lat // BLOCK * nz * nx
    half = lat // nc
    bf, f32 = jnp.bfloat16, jnp.float32

    per_half = half // BLOCK
    local_b = block_ids % (nc * per_half)
    shard = block_ids // (nc * per_half)
    place = (
        ((shard // nx) * nc + local_b // per_half) * nx + shard % nx
    ) * per_half + local_b % per_half

    per = CAP * HOMES
    rows_own = blocks // 2 // HOMES * per
    own_w = nx * half
    grid4 = (ny, nx, rows_own, LANES)
    w_enc, w_dec = (LANES, own_w), (own_w, LANES)
    scratch = {
        "held": pltpu.VMEM((blocks * per, LANES), f32),
        "rows": pltpu.VMEM((blocks * per, LANES), bf),
        "part": pltpu.VMEM(grid4, bf),
        "codes": pltpu.VMEM(grid4, bf),
        "pgrad": pltpu.VMEM(grid4, bf),
        "tok_all": pltpu.VMEM((HOMES, tok, LANES), bf),
        "pos_all": pltpu.VMEM((HOMES, 8, tok), jnp.int32),
        "enc_all": pltpu.VMEM((nz, nc) + w_enc, bf),
        "dec_all": pltpu.VMEM((nz, nc) + w_dec, bf),
        "slopes": pltpu.VMEM((rows_own, LANES), f32),
        "bias_all": pltpu.VMEM((nz, nx, lat // LANES, LANES), f32),
        "first": pltpu.VMEM((2, 3, 4, rows_own // 2, LANES), bf),
        "second": pltpu.VMEM((2, 3, rows_own // 2, LANES), f32),
        "total": pltpu.VMEM((2, 4, rows_own // 2, LANES), f32),
    }
    for name, shape in (("d_", w_dec), ("e_", w_enc)):
        scratch[name + "out"] = pltpu.VMEM((2,) + shape, f32)
        scratch[name + "half"] = pltpu.VMEM((nz,) + shape, f32)
        scratch[name + "narrow"] = pltpu.VMEM((nz,) + shape, bf)
        lead = (nz - 1,) if name == "d_" else (2, nz // 2)
        scratch[name + "z_in"] = pltpu.VMEM(lead + shape, bf)
        scratch[name + "sums"] = pltpu.VMEM(shape, f32)
    for name, shape in (
        ("w", (2, 2, 2)), ("b", (3,)), ("t", (15,)), ("p", (15,)), ("er", (2, 4, 2)), ("ec", (8,)),
        ("dr", (2, 4, 2)), ("dc", (8,)), ("bz", (7,)), ("s", (2, 4, 2, 3)), ("gr", (2, 4)), ("c", (2, 8)), ("z", (1, 7)),
    ):
        scratch[name + "send"] = sems(*shape)
        scratch[name + "recv"] = sems(*((2, 4) if name == "w" else shape))
    scratch.update(lsem=sems(2), hsend=sems(2, 4), hrecv=sems(2, 2, 2))

    vmem = pl.BlockSpec(memory_space=pltpu.VMEM)
    enc_share, dec_share = pl.pallas_call(
        functools.partial(train_kernel, tuple(scratch)),
        out_shape=[jax.ShapeDtypeStruct((part, lat), f32), jax.ShapeDtypeStruct((lat, part), f32)],
        in_specs=[pl.BlockSpec(memory_space=pl.ANY)] + [vmem] * 4,
        out_specs=[vmem] * 2,
        scratch_shapes=list(scratch.values()),
        compiler_params=pltpu.CompilerParams(
            collective_id=1, has_side_effects=True, vmem_limit_bytes=VMEM
        ),
        name="train",
    )(tokens, place.T, enc_master.astype(bf), dec_master.astype(bf), enc_bias.reshape(-1, LANES))
    enc_new, enc_first_new, enc_second_new = adam(enc_master, enc_share, enc_first, enc_second)
    dec_new, dec_first_new, dec_second_new = adam(dec_master, dec_share, dec_first, dec_second)
    return (enc_new, dec_new, enc_first_new, enc_second_new, dec_first_new, dec_second_new)


def solution(mesh):
    grid = Mesh(mesh.devices.reshape(8, 4, 4, 2), ("z", "x", "y", "c"))
    lat, rep = ("z", "x"), REP
    tok = P(rep + lat, None)
    enc, dec = P(rep, lat), P(lat, rep)
    return jax.shard_map(
        local,
        mesh=grid,
        in_specs=(tok, tok, P(lat), enc, dec, enc, enc, dec, dec),
        out_specs=(enc, dec, enc, enc, dec, dec),
        check_vma=False,
    )
```

```python
import functools

import jax
import jax.numpy as jnp
from jax import lax
from jax.experimental import pallas as pl
from jax.experimental.pallas import tpu as pltpu
from jax.sharding import Mesh, PartitionSpec as P

BLOCK = 64
CAP = 5
LANES = 128
HOMES = 16
VMEM = 62 * 2**20

learn_rate = 0.001
adam_eps = 1e-08
first_fix = 1.0 - 0.9**10
second_fix = 1.0 - 0.95**10

REP = ("y", "c")
CHIPS = ("y", "x")


def adam(master, gradient, first, second):
    first_new = 0.9 * first + 0.1 * gradient
    second_new = 0.95 * second + 0.05 * gradient * gradient
    update = first_new / first_fix / (jnp.sqrt(second_new / second_fix) + adam_eps)
    return (master - learn_rate * update, first_new, second_new)


def dot(a, b, ca, cb):
    return lax.dot_general(a, b, (((ca,), (cb,)), ((), ())), preferred_element_type=jnp.float32)


def low_lanes(shape):
    return lax.broadcasted_iota(jnp.int32, shape, 1) < BLOCK


def split_pair(pair):
    low = low_lanes(pair.shape)
    zero = jnp.zeros_like(pair)
    return jnp.concatenate([jnp.where(low, pair, zero), jnp.where(low, zero, pair)], axis=0)


def join_pair(both):
    half = both.shape[0] // 2
    return jnp.where(low_lanes((half, LANES)), both[:half], both[half:])


def slot_onehot(pos_ref, home, slot, blocks, tok):
    rows = (lax.broadcasted_iota(jnp.int32, (blocks, tok), 0) + slot * blocks).astype(jnp.int16)
    first = pos_ref[home, 0:1, :].astype(jnp.int16)
    second = pos_ref[home, 1:2, :].astype(jnp.int16)
    one, zero = jnp.ones((), jnp.bfloat16), jnp.zeros((), jnp.bfloat16)
    return jnp.where((rows == first) | (rows == second), one, zero)


MESH = pl.DeviceIdType.MESH


def axis_ids():
    return {a: lax.axis_index(a) for a in ("z", "x", "y", "c")}


def step(ids, axis, d):
    n = lax.axis_size(axis)
    return lax.rem(ids[axis] + (d + n), n)


def meet(peers):
    barrier = pltpu.get_barrier_semaphore()
    for peer in peers:
        pl.semaphore_signal(barrier, inc=1, device_id=peer, device_id_type=MESH)
    pl.semaphore_wait(barrier, len(peers))


def send(src, dst, ssem, rsem, peer):
    copy = pltpu.make_async_remote_copy(
        src_ref=src, dst_ref=dst, send_sem=ssem, recv_sem=rsem, device_id=peer, device_id_type=MESH
    )
    copy.start()
    return copy


def finish(copies):
    for copy in copies:
        copy.wait()


def ring_peers(ids, axis):
    return [{axis: step(ids, axis, d)} for d in range(1, lax.axis_size(axis))]


CHAINS = 2


def reduce_share(ids, part, out, first, second, total, ssem, rsem, produce, middle, hooks):
    x, y = ids["x"], ids["y"]
    count = part.shape[2] // CHAINS
    chains = range(CHAINS)
    cut = [pl.ds(h * count, count) for h in chains]

    def start(k, h, d, src, dst, peer):
        return send(src, dst, ssem.at[k, h, d - 1], rsem.at[k, h, d - 1], peer)

    def stage(k, h, pairs):
        return [start(k, h, d, *pairs(h, d)) for d in (1, 3, 2)]

    def one(h, d):
        axis = "xy"[h % 2]
        t = step(ids, axis, d)
        src = part.at[:, t, cut[h]] if axis == "x" else part.at[t, :, cut[h]]
        return src, first.at[h, d - 1], {axis: t}

    def two(h, d):
        axis = "yx"[h % 2]
        t = step(ids, axis, d)
        return total.at[h, t], second.at[h, d - 1], {axis: t}

    def three(h, d):
        axis = "yx"[h % 2]
        mine = out.at[y, x, cut[h]]
        return mine, mine, {axis: step(ids, axis, d)}

    def four(h, d):
        axis = "xy"[h % 2]
        mine = out.at[:, x, cut[h]] if axis == "x" else out.at[y, :, cut[h]]
        return mine, mine, {axis: step(ids, axis, d)}

    sent = [[] for h in chains]
    for pair in range(0, CHAINS, 2):
        for d in (1, 3, 2):
            for h in (pair, pair + 1):
                produce(h, d)
                sent[h].append(start(0, h, d, *one(h, d)))
    for h in chains:
        produce(h, 0)
    hooks[0]()
    for h in chains:
        finish(sent[h])
        for k in range(4):
            own = part.at[k, x, cut[h]] if h % 2 == 0 else part.at[y, k, cut[h]]
            acc = own[...].astype(jnp.float32)
            for d in range(3):
                acc += first[h, d, k].astype(jnp.float32)
            total[h, k] = acc
        sent[h] = stage(1, h, two)
    hooks[1]()
    for h in chains:
        finish(sent[h])
        acc = total[h, x if h % 2 else y]
        for d in range(3):
            acc += second[h, d]
        middle(h, acc)
        sent[h] = stage(2, h, three)
    hooks[2]()
    for h in chains:
        finish(sent[h])
        sent[h] = stage(3, h, four)
    hooks[3]()
    for h in chains:
        finish(sent[h])


def gelu_parts(v):
    a, b = 0.7978845608028654, 0.044715
    t = jnp.tanh(a * (v + b * (v * v * v)))
    value = 0.5 * v * (1.0 + t)
    slope = 0.5 * (1.0 + t) + 0.5 * v * (1.0 - t * t) * (a * (1.0 + 3.0 * b * (v * v)))
    return value, slope


class ZRing:
    def __init__(self, ids, buf, rsend, rrecv, csend, crecv):
        self.ids, self.buf, self.c = ids, buf, ids["c"]
        self.sems, self.core = (rsend, rrecv), (csend, crecv)
        self.half = buf.shape[2] // 2
        self.sent, self.over = {}, []

    def launch(self, k, s):
        for way, sign in ((0, 1), (1, -1)):
            if k < 3 or s == way:
                zz = step(self.ids, "z", -sign * k)
                piece = self.buf.at[zz, self.c, pl.ds(s * self.half, self.half)]
                sems = [sem.at[way, k, s] for sem in self.sems]
                self.sent[way, k, s] = send(piece, piece, *sems, {"z": step(self.ids, "z", sign)})

    def share(self, zz):
        n = len(self.over)
        block = self.buf.at[zz, self.c]
        sems = [sem.at[n] for sem in self.core]
        self.over.append(send(block, block, *sems, {"c": 1 - self.c}))

    def begin(self):
        for s in range(2):
            self.launch(0, s)
        self.share(self.ids["z"])

    def arrive(self, k):
        for s in range(2):
            for way in range(2):
                if k < 4 or s == way:
                    self.sent[way, k - 1, s].wait_recv()
            if k < 4:
                self.launch(k, s)
        self.share(step(self.ids, "z", -k))
        if k < 4:
            self.share(step(self.ids, "z", k))

    def end(self):
        for copy in self.sent.values():
            copy.wait_send()
        finish(self.over)


def swap_homes(ids, items, ssem, rsem):
    started = []
    for n, r, src, dst, tx, tc in items:
        own = (tx == ids["x"]) & (tc == ids["c"])
        copy = pltpu.make_async_remote_copy(
            src_ref=src, dst_ref=dst, send_sem=ssem.at[n], recv_sem=rsem.at[r],
            device_id={"x": tx, "c": tc}, device_id_type=MESH,
        )
        keep = pltpu.make_async_copy(src, dst, rsem.at[r])

        @pl.when(own)
        def _():
            keep.start()

        @pl.when(jnp.logical_not(own))
        def _():
            copy.start()

        started.append((own, copy))
    return started


def sent_homes(started):
    for own, copy in started:
        @pl.when(jnp.logical_not(own))
        def _():
            copy.wait_send()


def landed(dst, sem):
    pltpu.make_async_copy(dst, dst, sem).wait()


PLANE = (
    (1, 0), (0, 1), (3, 0), (0, 3), (1, 1), (3, 3), (1, 3), (3, 1),
    (2, 0), (0, 2), (1, 2), (2, 1), (3, 2), (2, 3), (2, 2),
)
NEAR = 8
FAR = (4, 3, 5, 2, 6, 1, 7, 0)
SLOTS = 4


def train_kernel(names, *refs):
    tokens, place, enc_wide, dec_wide, bias, enc_out, dec_out = refs[:7]
    v = dict(zip(names, refs[7:]))
    enc, dec = v["enc"], v["dec"]
    enc[...] = enc_wide[...].astype(jnp.bfloat16)
    dec[...] = dec_wide[...].astype(jnp.bfloat16)
    ids = axis_ids()
    x, y, z, c = ids["x"], ids["y"], ids["z"], ids["c"]
    me = y * 4 + x
    other = {"c": 1 - c}
    per = CAP * HOMES
    held, rows, part, codes, pgrad = v["held"], v["rows"], v["part"], v["codes"], v["pgrad"]
    tok_all, pos_all, enc_all, dec_all = v["tok_all"], v["pos_all"], v["enc_all"], v["dec_all"]
    slopes, bias_all = v["slopes"], v["bias_all"]
    tok = tok_all.shape[1]
    pairs = part.shape[2] // per
    blocks = HOMES * pairs * 2
    lat = dec.shape[0] // 2
    bf, f32 = jnp.bfloat16, jnp.float32

    peers = [{"y": step(ids, "y", a), "x": step(ids, "x", b)} for a, b in PLANE]
    crossed = [{"x": step(ids, "x", d), "c": 1 - c} for d in range(4)]
    meet(peers + crossed + ring_peers(ids, "z"))

    swaps = []
    for m in range(2):
        for i in range(2):
            for h in range(2):
                at = pl.ds(pl.multiple_of(x * lat, lat), lat)
                if m == 0:
                    src = enc.at[pl.ds(i * LANES, LANES), pl.ds(h * lat, lat)]
                    dst = enc_all.at[z, h, :, at]
                else:
                    src = dec.at[pl.ds(h * lat, lat), pl.ds(i * LANES, LANES)]
                    dst = dec_all.at[z, h, at]
                swaps.append(((m, i, h), (m, x), src, dst, 2 * c + i, h))
    swaps = swap_homes(ids, swaps, _At(v["wsend"]), _At(v["wrecv"]))
    bias_x = [
        send(bias, bias_all.at[z, x], v["bsend"].at[d - 1], v["brecv"].at[d - 1], {"x": step(ids, "x", d)})
        for d in range(1, 4)
    ]
    keep = [
        pltpu.make_async_copy(bias, bias_all.at[z, x], v["lsem"].at[0]),
        pltpu.make_async_copy(
            tokens.at[:, pl.ds(pl.multiple_of(me * LANES, LANES), LANES)], tok_all.at[me], v["lsem"].at[1]
        ),
    ]
    for copy in keep:
        copy.start()
    def send_tokens(numbers):
        copies = []
        for n in numbers:
            a, b = PLANE[n]
            t = step(ids, "y", a) * 4 + step(ids, "x", b)
            src = tokens.at[:, pl.ds(pl.multiple_of(t * LANES, LANES), LANES)]
            copies.append(send(src, tok_all.at[me], v["tsend"].at[n], v["trecv"].at[n], peers[n]))
        return copies

    near = send_tokens(range(NEAR))

    numbers = lax.broadcasted_iota(jnp.int32, (blocks, tok), 0)
    named = [numbers == place[k : k + 1, :] for k in range(2)]
    one, zero = jnp.ones((), f32), jnp.zeros((), f32)
    either = jnp.where(named[0] | named[1], one, zero).astype(bf)
    before = lax.broadcasted_iota(jnp.int32, (tok, tok), 0) < lax.broadcasted_iota(jnp.int32, (tok, tok), 1)
    count = dot(either, jnp.where(before, one, zero).astype(bf), 1, 0)
    pos_all[me] = jnp.zeros(pos_all.shape[1:], jnp.int32)
    for k in range(2):
        rank = jnp.sum(jnp.where(named[k], count, zero), axis=0, keepdims=True).astype(jnp.int32)
        pos_all[me, k : k + 1, :] = rank * blocks + place[k : k + 1, :]
    ranks = [
        send(pos_all.at[me], pos_all.at[me], v["psend"].at[n], v["precv"].at[n], peers[n]) for n in range(15)
    ]
    distant = send_tokens(range(NEAR, 15))

    ring = ZRing(ids, enc_all, v["ersend"], v["errecv"], v["ecsend"], v["ecrecv"])
    for src in range(4):
        landed(enc_all.at[z, c, :, pl.ds(src * lat, lat)], v["wrecv"].at[0, src])
    ring.begin()
    finish(bias_x)
    keep[0].wait()
    bias_z = [
        send(bias_all.at[z], bias_all.at[z], v["bzsend"].at[d - 1], v["bzrecv"].at[d - 1], {"z": step(ids, "z", d)})
        for d in range(1, 8)
    ]
    ring.arrive(1)
    ring.arrive(2)
    def gather(count, offsets):
        @pl.loop(0, count)
        def _(n):
            a, b = offsets(n)
            home = lax.rem(y + 4 - a, 4) * 4 + lax.rem(x + 4 - b, 4)
            mine = tok_all[home]
            for slot in range(CAP):
                picked = dot(slot_onehot(pos_all, home, slot, blocks, tok), mine, 1, 0)
                held[pl.ds(slot * HOMES + home, blocks, per), :] = picked

    def skip_two(n):
        return n + lax.div(n, 2)

    finish(near + ranks[:NEAR])
    keep[1].wait()
    gather(NEAR + 1, lambda n: (skip_two(lax.div(n, 3)), skip_two(lax.rem(n, 3))))
    ring.arrive(3)
    finish(distant + ranks[NEAR:])
    gather(4, lambda n: (2, n))
    gather(3, lambda n: (skip_two(n), 2))
    ring.arrive(4)
    around = ZRing(ids, dec_all, v["drsend"], v["drrecv"], v["dcsend"], v["dcrecv"])
    for src in range(4):
        landed(dec_all.at[z, c, pl.ds(src * lat, lat)], v["wrecv"].at[1, src])
    around.begin()
    finish(bias_z)
    ring.end()

    def pair_rows(q, j):
        return pl.ds(pl.multiple_of((q * pairs + j) * 2 * per, 2 * per), 2 * per)

    def code_rows(j):
        return pl.ds(pl.multiple_of(j * per, per), per)

    def weight_rows(j):
        return pl.ds(pl.multiple_of(j * LANES, LANES), LANES)

    def own_pairs(ref, q, j):
        return ref.at[lax.div(q, 4), lax.rem(q, 4), code_rows(j), :]

    def groups(body):
        def produce(h, d):
            t = step(ids, "xy"[h % 2], d)

            @pl.loop(0, 4)
            def _(k):
                q = 4 * k + t if h % 2 == 0 else 4 * t + k
                for j in range(pairs // CHAINS):
                    body(q, h * (pairs // CHAINS) + j)

        return produce

    def encode(q, j):
        mine = held[pair_rows(q, j), :].astype(bf)
        rows[pair_rows(q, j), :] = mine
        weight = enc_all[lax.div(q, 2), lax.rem(q, 2), :, weight_rows(j)]
        own_pairs(part, q, j)[...] = join_pair(dot(mine, weight, 1, 0)).astype(bf)

    def activate(h, acc):
        for k in range(pairs // CHAINS):
            j = h * (pairs // CHAINS) + k
            shift = bias_all[lax.div(me, 2), j // 2, pl.ds(2 * lax.rem(me, 2) + j % 2, 1), :]
            value, slope = gelu_parts(acc[k * per : (k + 1) * per] + shift)
            codes[y, x, j * per : (j + 1) * per] = value.astype(bf)
            slopes[j * per : (j + 1) * per, :] = slope

    stages = [v[k] for k in ("first", "second", "total")]
    reduce_share(
        ids, part, codes, *stages, v["ssend"].at[0], v["srecv"].at[0], groups(encode), activate,
        [lambda k=k: around.arrive(k) for k in range(1, 5)],
    )
    around.end()

    @pl.loop(0, HOMES)
    def _(q):
        for j in range(pairs):
            weight = dec_all[lax.div(q, 2), lax.rem(q, 2), weight_rows(j), :]
            held[pair_rows(q, j), :] = dot(split_pair(own_pairs(codes, q, j)[...]), weight, 1, 0)

    @pl.loop(0, HOMES, unroll=2)
    def _(home):
        hots = jnp.concatenate([slot_onehot(pos_all, home, slot, blocks, tok) for slot in range(CAP)], axis=0)
        at = [pl.ds(slot * HOMES + home, blocks, per) for slot in range(CAP)]
        some = jnp.concatenate([held[a, :].astype(bf) for a in at], axis=0)
        rebuilt = dot(some, hots, 0, 0)
        err = (rebuilt - tok_all[home].astype(f32).T).astype(bf)
        picked = dot(hots, err, 1, 1)
        for slot in range(CAP):
            held[at[slot], :] = picked[slot * blocks : (slot + 1) * blocks]

    def code_grad(q, j):
        err = held[pair_rows(q, j), :].astype(bf)
        weight = dec_all[lax.div(q, 2), lax.rem(q, 2), weight_rows(j), :]
        own_pairs(part, q, j)[...] = join_pair(dot(err, weight, 1, 1)).astype(bf)

    def dec_grad(q, j):
        err = held[pair_rows(q, j), :].astype(bf)
        return dot(split_pair(own_pairs(codes, q, j)[...]), err, 0, 0)

    def enc_grad(q, j):
        return dot(rows[pair_rows(q, j), :], split_pair(own_pairs(pgrad, q, j)[...]), 0, 0)

    def collect(m, grad, name, chain):
        out, half_in, narrow, z_in, sums = (v[name + k] for k in ("out", "half", "narrow", "z_in", "sums"))

        def slot(ref, j, *lead):
            return ref.at[(*lead, slice(None), weight_rows(j))] if m else ref.at[(*lead, weight_rows(j))]


        def cut_rows(way):
            cut = z_in.shape[2] // 2
            return pl.ds(way * cut, cut)

        def ring_on(d, n):
            ways = (0, 1) if d == 4 else (0,) if 0 < d < 4 else (1,) if d else ()
            for way in ways:
                k = min(d, 8 - d)
                src, dst = narrow.at[n % SLOTS], z_in.at[way, k - 1]
                if k == 4:
                    src, dst = narrow.at[n % SLOTS, cut_rows(way)], z_in.at[way, 3, cut_rows(way)]
                sems = [v[e].at[m, way, k - 1] for e in ("grsend", "grrecv")]
                chain[way, k] = send(src, dst, *sems, {"z": step(ids, "z", 1 - 2 * way)})

        def pass_on(copy, d, t, n):
            copy.wait()
            if d and n >= SLOTS:
                freed = FAR[n - SLOTS]
                for way in range(2) if freed == 4 else [int(freed > 4)]:
                    chain.pop((way, min(freed, 8 - freed))).wait_send()
            way, k = (0, d) if d < 4 else (1, 8 - d)
            if d == 0:
                chain[0, 1].wait_recv()
                chain[1, 1].wait_recv()
            elif d != 4:
                chain[way, k + 1].wait_recv()
            for j in range(pairs):
                acc = grad(2 * t + c, j) + slot(half_in, j, t)[...]
                if d and d != 4:
                    came = slot(z_in, j, way, k)
                    if k == 3 and m == 0:
                        if (j >= pairs // 2) == (way == 1):
                            acc += came[...].astype(f32)
                    elif k == 3:
                        cut = acc.shape[0] // 2
                        lower, upper = acc[:cut], acc[cut:]
                        if way == 0:
                            lower += came[:cut].astype(f32)
                        else:
                            upper += came[cut:].astype(f32)
                        acc = jnp.concatenate([lower, upper], axis=0)
                    else:
                        acc += came[...].astype(f32)
                if d == 0:
                    acc += slot(z_in, j, 0, 0)[...].astype(f32) + slot(z_in, j, 1, 0)[...].astype(f32)
                if d == 0:
                    slot(sums, j)[...] = acc
                else:
                    slot(narrow, j, n % SLOTS)[...] = acc.astype(bf)
            ring_on(d, n)

        last = None
        for k, d in enumerate(FAR):
            t = step(ids, "z", d)
            for j in range(pairs):
                slot(out, j, k % 2)[...] = grad(2 * t + 1 - c, j)
            copy = send(out.at[k % 2], half_in.at[t], v["csend"].at[m, k], v["crecv"].at[m, k], other)
            if last is not None:
                pass_on(*last)
            last = (copy, d, t, k)
            yield
        pass_on(*last)
        yield

    dec_chain, enc_chain = {}, {}
    dec_steps = collect(0, dec_grad, "d_", dec_chain)

    def advance(n):
        return lambda: [next(dec_steps) for _ in range(n)]

    def multiply(h, acc):
        at = pl.ds(h * acc.shape[0], acc.shape[0])
        pgrad[y, x, at] = (acc * slopes[at, :]).astype(bf)

    reduce_share(
        ids, part, pgrad, *stages, v["ssend"].at[1], v["srecv"].at[1], groups(code_grad), multiply,
        [advance(4), advance(2), advance(2), advance(1)],
    )
    for _ in collect(1, enc_grad, "e_", enc_chain):
        pass

    homes = []
    for m, name, chain, dst in ((0, "d_", dec_chain, dec_out), (1, "e_", enc_chain, enc_out)):
        sums = v[name + "sums"]
        for copy in chain.values():
            copy.wait_send()
        at = pl.ds(pl.multiple_of(c * lat, lat), lat)
        lanes = pl.ds(pl.multiple_of(lax.rem(x, 2) * LANES, LANES), LANES)
        items = []
        for t in range(4):
            piece = pl.ds(t * lat, lat)
            if m == 0:
                src, to = sums.at[piece], dst.at[at, lanes]
            else:
                src, to = sums.at[:, piece], dst.at[lanes, at]
            items.append(((m, t), (m, c, lax.rem(x, 2)), src, to, t, lax.div(x, 2)))
        homes += swap_homes(ids, items, _At(v["hsend"]), _At(v["hrecv"]))
    for m, dst in ((0, dec_out), (1, enc_out)):
        for h in range(2):
            for i in range(2):
                at, lanes = pl.ds(h * lat, lat), pl.ds(i * LANES, LANES)
                landed(dst.at[at, lanes] if m == 0 else dst.at[lanes, at], v["hrecv"].at[m, h, i])
    sent_homes(swaps)
    sent_homes(homes)


class _At:
    def __init__(self, ref):
        self.ref = ref

    @property
    def at(self):
        return self

    def __getitem__(self, index):
        return self.ref.at[index]


def sems(*shape):
    return pltpu.SemaphoreType.DMA(shape)


def local(
    tokens,
    block_ids,
    enc_bias,
    enc_master,
    dec_master,
    enc_first,
    enc_second,
    dec_first,
    dec_second,
):
    nz, nx = lax.axis_size("z"), lax.axis_size("x")
    ny, nc = lax.axis_size("y"), lax.axis_size("c")
    tok, width = tokens.shape
    lat, part = dec_master.shape
    blocks = lat // BLOCK * nz * nx
    half = lat // nc
    bf, f32 = jnp.bfloat16, jnp.float32

    per_half = half // BLOCK
    local_b = block_ids % (nc * per_half)
    shard = block_ids // (nc * per_half)
    place = (
        ((shard // nx) * nc + local_b // per_half) * nx + shard % nx
    ) * per_half + local_b % per_half

    per = CAP * HOMES
    rows_own = blocks // 2 // HOMES * per
    own_w = nx * half
    grid4 = (ny, nx, rows_own, LANES)
    w_enc, w_dec = (LANES, own_w), (own_w, LANES)
    scratch = {
        "enc": pltpu.VMEM((part, lat), bf),
        "dec": pltpu.VMEM((lat, part), bf),
        "held": pltpu.VMEM((blocks * per, LANES), f32),
        "rows": pltpu.VMEM((blocks * per, LANES), bf),
        "part": pltpu.VMEM(grid4, bf),
        "codes": pltpu.VMEM(grid4, bf),
        "pgrad": pltpu.VMEM(grid4, bf),
        "tok_all": pltpu.VMEM((HOMES, tok, LANES), bf),
        "pos_all": pltpu.VMEM((HOMES, 8, tok), jnp.int32),
        "enc_all": pltpu.VMEM((nz, nc) + w_enc, bf),
        "dec_all": pltpu.VMEM((nz, nc) + w_dec, bf),
        "slopes": pltpu.VMEM((rows_own, LANES), f32),
        "bias_all": pltpu.VMEM((nz, nx, lat // LANES, LANES), f32),
        "first": pltpu.VMEM((CHAINS, 3, 4, rows_own // CHAINS, LANES), bf),
        "second": pltpu.VMEM((CHAINS, 3, rows_own // CHAINS, LANES), f32),
        "total": pltpu.VMEM((CHAINS, 4, rows_own // CHAINS, LANES), f32),
    }
    for name, shape in (("d_", w_dec), ("e_", w_enc)):
        scratch[name + "out"] = pltpu.VMEM((2,) + shape, f32)
        scratch[name + "half"] = pltpu.VMEM((nz,) + shape, f32)
        scratch[name + "narrow"] = pltpu.VMEM((SLOTS,) + shape, bf)
        scratch[name + "z_in"] = pltpu.VMEM((2, nz // 2) + shape, bf)
        scratch[name + "sums"] = pltpu.VMEM(shape, f32)
    for name, shape in (
        ("w", (2, 2, 2)), ("b", (3,)), ("t", (15,)), ("p", (15,)), ("er", (2, 4, 2)), ("ec", (8,)),
        ("dr", (2, 4, 2)), ("dc", (8,)), ("bz", (7,)), ("s", (2, 4, CHAINS, 3)), ("gr", (2, 2, 4)), ("c", (2, 8)),
    ):
        scratch[name + "send"] = sems(*shape)
        scratch[name + "recv"] = sems(*((2, 4) if name == "w" else shape))
    scratch.update(lsem=sems(2), hsend=sems(2, 4), hrecv=sems(2, 2, 2))

    vmem = pl.BlockSpec(memory_space=pltpu.VMEM)
    enc_share, dec_share = pl.pallas_call(
        functools.partial(train_kernel, tuple(scratch)),
        out_shape=[jax.ShapeDtypeStruct((part, lat), f32), jax.ShapeDtypeStruct((lat, part), f32)],
        in_specs=[pl.BlockSpec(memory_space=pl.ANY)] + [vmem] * 4,
        out_specs=[vmem] * 2,
        scratch_shapes=list(scratch.values()),
        compiler_params=pltpu.CompilerParams(
            collective_id=1, has_side_effects=True, vmem_limit_bytes=VMEM
        ),
        name="train",
    )(tokens, place.T, enc_master, dec_master, enc_bias.reshape(-1, LANES))
    enc_new, enc_first_new, enc_second_new = adam(enc_master, enc_share, enc_first, enc_second)
    dec_new, dec_first_new, dec_second_new = adam(dec_master, dec_share, dec_first, dec_second)
    return (enc_new, dec_new, enc_first_new, enc_second_new, dec_first_new, dec_second_new)


def solution(mesh):
    grid = Mesh(mesh.devices.reshape(8, 4, 4, 2), ("z", "x", "y", "c"))
    lat, rep = ("z", "x"), REP
    tok = P(rep + lat, None)
    enc, dec = P(rep, lat), P(lat, rep)
    return jax.shard_map(
        local,
        mesh=grid,
        in_specs=(tok, tok, P(lat), enc, dec, enc, enc, dec, dec),
        out_specs=(enc, dec, enc, enc, dec, dec),
        check_vma=False,
    )
```

```python
import functools

import jax
import jax.numpy as jnp
from jax import lax
from jax.experimental import pallas as pl
from jax.experimental.pallas import tpu as pltpu
from jax.sharding import Mesh, PartitionSpec as P

BLOCK = 64
CAP = 5
LANES = 128
HOMES = 16
VMEM = 62 * 2**20

learn_rate = 0.001
adam_eps = 1e-08
first_fix = 1.0 - 0.9**10
second_fix = 1.0 - 0.95**10

REP = ("y", "c")
CHIPS = ("y", "x")


def adam(master, gradient, first, second):
    first_new = 0.9 * first + 0.1 * gradient
    second_new = 0.95 * second + 0.05 * gradient * gradient
    update = first_new / first_fix / (jnp.sqrt(second_new / second_fix) + adam_eps)
    return (master - learn_rate * update, first_new, second_new)


def dot(a, b, ca, cb):
    return lax.dot_general(a, b, (((ca,), (cb,)), ((), ())), preferred_element_type=jnp.float32)


def low_lanes(shape):
    return lax.broadcasted_iota(jnp.int32, shape, 1) < BLOCK


def split_pair(pair):
    low = low_lanes(pair.shape)
    zero = jnp.zeros_like(pair)
    return jnp.concatenate([jnp.where(low, pair, zero), jnp.where(low, zero, pair)], axis=0)


def join_pair(both):
    half = both.shape[0] // 2
    return jnp.where(low_lanes((half, LANES)), both[:half], both[half:])


def slot_onehot(pos_ref, home, slot, blocks, tok):
    rows = (lax.broadcasted_iota(jnp.int32, (blocks, tok), 0) + slot * blocks).astype(jnp.int16)
    first = pos_ref[home, 0:1, :].astype(jnp.int16)
    second = pos_ref[home, 1:2, :].astype(jnp.int16)
    one, zero = jnp.ones((), jnp.bfloat16), jnp.zeros((), jnp.bfloat16)
    return jnp.where((rows == first) | (rows == second), one, zero)


MESH = pl.DeviceIdType.MESH


def axis_ids():
    return {a: lax.axis_index(a) for a in ("z", "x", "y", "c")}


def step(ids, axis, d):
    n = lax.axis_size(axis)
    return lax.rem(ids[axis] + (d + n), n)


def meet(peers):
    barrier = pltpu.get_barrier_semaphore()
    for peer in peers:
        pl.semaphore_signal(barrier, inc=1, device_id=peer, device_id_type=MESH)
    pl.semaphore_wait(barrier, len(peers))


def send(src, dst, ssem, rsem, peer):
    copy = pltpu.make_async_remote_copy(
        src_ref=src, dst_ref=dst, send_sem=ssem, recv_sem=rsem, device_id=peer, device_id_type=MESH
    )
    copy.start()
    return copy


def finish(copies):
    for copy in copies:
        copy.wait()


def ring_peers(ids, axis):
    return [{axis: step(ids, axis, d)} for d in range(1, lax.axis_size(axis))]


CHAINS = 2


def reduce_share(ids, part, out, first, second, total, ssem, rsem, produce, middle, hooks):
    x, y = ids["x"], ids["y"]
    count = part.shape[2] // CHAINS
    chains = range(CHAINS)
    cut = [pl.ds(h * count, count) for h in chains]

    def start(k, h, d, src, dst, peer):
        return send(src, dst, ssem.at[k, h, d - 1], rsem.at[k, h, d - 1], peer)

    def stage(k, h, pairs):
        return [start(k, h, d, *pairs(h, d)) for d in (1, 3, 2)]

    def one(h, d):
        axis = "xy"[h % 2]
        t = step(ids, axis, d)
        src = part.at[:, t, cut[h]] if axis == "x" else part.at[t, :, cut[h]]
        return src, first.at[h, d - 1], {axis: t}

    def two(h, d):
        axis = "yx"[h % 2]
        t = step(ids, axis, d)
        return total.at[h, t], second.at[h, d - 1], {axis: t}

    def three(h, d):
        axis = "yx"[h % 2]
        mine = out.at[y, x, cut[h]]
        return mine, mine, {axis: step(ids, axis, d)}

    def four(h, d):
        axis = "xy"[h % 2]
        mine = out.at[:, x, cut[h]] if axis == "x" else out.at[y, :, cut[h]]
        return mine, mine, {axis: step(ids, axis, d)}

    sent = [[] for h in chains]
    for pair in range(0, CHAINS, 2):
        for d in (1, 3, 2):
            for h in (pair, pair + 1):
                produce(h, d)
                sent[h].append(start(0, h, d, *one(h, d)))
    for h in chains:
        produce(h, 0)
    hooks[0]()
    for h in chains:
        finish(sent[h])
        for k in range(4):
            own = part.at[k, x, cut[h]] if h % 2 == 0 else part.at[y, k, cut[h]]
            acc = own[...].astype(jnp.float32)
            for d in range(3):
                acc += first[h, d, k].astype(jnp.float32)
            total[h, k] = acc
        sent[h] = stage(1, h, two)
    hooks[1]()
    for h in chains:
        finish(sent[h])
        acc = total[h, x if h % 2 else y]
        for d in range(3):
            acc += second[h, d]
        middle(h, acc)
        sent[h] = stage(2, h, three)
    hooks[2]()
    for h in chains:
        finish(sent[h])
        sent[h] = stage(3, h, four)
    hooks[3]()
    for h in chains:
        finish(sent[h])


def gelu_parts(v):
    a, b = 0.7978845608028654, 0.044715
    t = jnp.tanh(a * (v + b * (v * v * v)))
    value = 0.5 * v * (1.0 + t)
    slope = 0.5 * (1.0 + t) + 0.5 * v * (1.0 - t * t) * (a * (1.0 + 3.0 * b * (v * v)))
    return value, slope


class ZRing:
    def __init__(self, ids, buf, rsend, rrecv, csend, crecv):
        self.ids, self.buf, self.c = ids, buf, ids["c"]
        self.sems, self.core = (rsend, rrecv), (csend, crecv)
        self.half = buf.shape[2] // 2
        self.sent, self.over = {}, []

    def launch(self, k, s):
        for way, sign in ((0, 1), (1, -1)):
            if k < 3 or s == way:
                zz = step(self.ids, "z", -sign * k)
                piece = self.buf.at[zz, self.c, pl.ds(s * self.half, self.half)]
                sems = [sem.at[way, k, s] for sem in self.sems]
                self.sent[way, k, s] = send(piece, piece, *sems, {"z": step(self.ids, "z", sign)})

    def share(self, zz):
        n = len(self.over)
        block = self.buf.at[zz, self.c]
        sems = [sem.at[n] for sem in self.core]
        self.over.append(send(block, block, *sems, {"c": 1 - self.c}))

    def begin(self):
        for s in range(2):
            self.launch(0, s)
        self.share(self.ids["z"])

    def arrive(self, k):
        for s in range(2):
            for way in range(2):
                if k < 4 or s == way:
                    self.sent[way, k - 1, s].wait_recv()
            if k < 4:
                self.launch(k, s)
        self.share(step(self.ids, "z", -k))
        if k < 4:
            self.share(step(self.ids, "z", k))

    def end(self):
        for copy in self.sent.values():
            copy.wait_send()
        finish(self.over)


def swap_homes(ids, items, ssem, rsem):
    started = []
    for n, r, src, dst, tx, tc in items:
        own = (tx == ids["x"]) & (tc == ids["c"])
        copy = pltpu.make_async_remote_copy(
            src_ref=src, dst_ref=dst, send_sem=ssem.at[n], recv_sem=rsem.at[r],
            device_id={"x": tx, "c": tc}, device_id_type=MESH,
        )
        keep = pltpu.make_async_copy(src, dst, rsem.at[r])

        @pl.when(own)
        def _():
            keep.start()

        @pl.when(jnp.logical_not(own))
        def _():
            copy.start()

        started.append((own, copy))
    return started


def sent_homes(started):
    for own, copy in started:
        @pl.when(jnp.logical_not(own))
        def _():
            copy.wait_send()


def landed(dst, sem):
    pltpu.make_async_copy(dst, dst, sem).wait()


PLANE = (
    (1, 0), (0, 1), (3, 0), (0, 3), (1, 1), (3, 3), (1, 3), (3, 1),
    (2, 0), (0, 2), (1, 2), (2, 1), (3, 2), (2, 3), (2, 2),
)
NEAR = 8
FAR = (4, 3, 5, 2, 6, 1, 7, 0)
SLOTS = 4


def train_kernel(names, *refs):
    tokens, place, enc_wide, dec_wide, bias, enc_out, dec_out = refs[:7]
    v = dict(zip(names, refs[7:]))
    enc, dec = v["enc"], v["dec"]
    enc[...] = enc_wide[...].astype(jnp.bfloat16)
    dec[...] = dec_wide[...].astype(jnp.bfloat16)
    ids = axis_ids()
    x, y, z, c = ids["x"], ids["y"], ids["z"], ids["c"]
    me = y * 4 + x
    other = {"c": 1 - c}
    per = CAP * HOMES
    held, rows, part, codes, pgrad = v["held"], v["rows"], v["part"], v["codes"], v["pgrad"]
    tok_all, pos_all, enc_all, dec_all = v["tok_all"], v["pos_all"], v["enc_all"], v["dec_all"]
    slopes, bias_all = v["slopes"], v["bias_all"]
    tok = tok_all.shape[1]
    pairs = part.shape[2] // per
    blocks = HOMES * pairs * 2
    lat = dec.shape[0] // 2
    bf, f32 = jnp.bfloat16, jnp.float32

    peers = [{"y": step(ids, "y", a), "x": step(ids, "x", b)} for a, b in PLANE]
    crossed = [{"x": step(ids, "x", d), "c": 1 - c} for d in range(4)]
    meet(peers + crossed + ring_peers(ids, "z"))

    swaps = []
    for m in range(2):
        for i in range(2):
            for h in range(2):
                at = pl.ds(pl.multiple_of(x * lat, lat), lat)
                if m == 0:
                    src = enc.at[pl.ds(i * LANES, LANES), pl.ds(h * lat, lat)]
                    dst = enc_all.at[z, h, :, at]
                else:
                    src = dec.at[pl.ds(h * lat, lat), pl.ds(i * LANES, LANES)]
                    dst = dec_all.at[z, h, at]
                swaps.append(((m, i, h), (m, x), src, dst, 2 * c + i, h))
    swaps = swap_homes(ids, swaps, _At(v["wsend"]), _At(v["wrecv"]))
    bias_x = [
        send(bias, bias_all.at[z, x], v["bsend"].at[d - 1], v["brecv"].at[d - 1], {"x": step(ids, "x", d)})
        for d in range(1, 4)
    ]
    keep = [
        pltpu.make_async_copy(bias, bias_all.at[z, x], v["lsem"].at[0]),
        pltpu.make_async_copy(
            tokens.at[:, pl.ds(pl.multiple_of(me * LANES, LANES), LANES)], tok_all.at[me], v["lsem"].at[1]
        ),
    ]
    for copy in keep:
        copy.start()
    def send_tokens(numbers):
        copies = []
        for n in numbers:
            a, b = PLANE[n]
            t = step(ids, "y", a) * 4 + step(ids, "x", b)
            src = tokens.at[:, pl.ds(pl.multiple_of(t * LANES, LANES), LANES)]
            copies.append(send(src, tok_all.at[me], v["tsend"].at[n], v["trecv"].at[n], peers[n]))
        return copies

    near = send_tokens(range(NEAR))

    numbers = lax.broadcasted_iota(jnp.int32, (blocks, tok), 0)
    named = [numbers == place[k : k + 1, :] for k in range(2)]
    one, zero = jnp.ones((), f32), jnp.zeros((), f32)
    either = jnp.where(named[0] | named[1], one, zero).astype(bf)
    before = lax.broadcasted_iota(jnp.int32, (tok, tok), 0) < lax.broadcasted_iota(jnp.int32, (tok, tok), 1)
    count = dot(either, jnp.where(before, one, zero).astype(bf), 1, 0)
    pos_all[me] = jnp.zeros(pos_all.shape[1:], jnp.int32)
    for k in range(2):
        rank = jnp.sum(jnp.where(named[k], count, zero), axis=0, keepdims=True).astype(jnp.int32)
        pos_all[me, k : k + 1, :] = rank * blocks + place[k : k + 1, :]
    ranks = [
        send(pos_all.at[me], pos_all.at[me], v["psend"].at[n], v["precv"].at[n], peers[n]) for n in range(15)
    ]
    distant = send_tokens(range(NEAR, 15))

    ring = ZRing(ids, enc_all, v["ersend"], v["errecv"], v["ecsend"], v["ecrecv"])
    for src in range(4):
        landed(enc_all.at[z, c, :, pl.ds(src * lat, lat)], v["wrecv"].at[0, src])
    ring.begin()
    finish(bias_x)
    keep[0].wait()
    bias_z = [
        send(bias_all.at[z], bias_all.at[z], v["bzsend"].at[d - 1], v["bzrecv"].at[d - 1], {"z": step(ids, "z", d)})
        for d in range(1, 8)
    ]
    ring.arrive(1)
    ring.arrive(2)
    def gather(count, offsets):
        @pl.loop(0, count, unroll=count if count < 5 else 3)
        def _(n):
            a, b = offsets(n)
            home = lax.rem(y + 4 - a, 4) * 4 + lax.rem(x + 4 - b, 4)
            mine = tok_all[home]
            for slot in range(CAP):
                picked = dot(slot_onehot(pos_all, home, slot, blocks, tok), mine, 1, 0)
                held[pl.ds(slot * HOMES + home, blocks, per), :] = picked

    def skip_two(n):
        return n + lax.div(n, 2)

    finish(near + ranks[:NEAR])
    keep[1].wait()
    gather(NEAR + 1, lambda n: (skip_two(lax.div(n, 3)), skip_two(lax.rem(n, 3))))
    ring.arrive(3)
    finish(distant + ranks[NEAR:])
    gather(4, lambda n: (2, n))
    gather(3, lambda n: (skip_two(n), 2))
    ring.arrive(4)
    around = ZRing(ids, dec_all, v["drsend"], v["drrecv"], v["dcsend"], v["dcrecv"])
    for src in range(4):
        landed(dec_all.at[z, c, pl.ds(src * lat, lat)], v["wrecv"].at[1, src])
    around.begin()
    finish(bias_z)
    ring.end()

    def pair_rows(q, j):
        return pl.ds(pl.multiple_of((q * pairs + j) * 2 * per, 2 * per), 2 * per)

    def code_rows(j):
        return pl.ds(pl.multiple_of(j * per, per), per)

    def weight_rows(j):
        return pl.ds(pl.multiple_of(j * LANES, LANES), LANES)

    def own_pairs(ref, q, j):
        return ref.at[lax.div(q, 4), lax.rem(q, 4), code_rows(j), :]

    def groups(body):
        def produce(h, d):
            t = step(ids, "xy"[h % 2], d)

            @pl.loop(0, 4)
            def _(k):
                q = 4 * k + t if h % 2 == 0 else 4 * t + k
                for j in range(pairs // CHAINS):
                    body(q, h * (pairs // CHAINS) + j)

        return produce

    def encode(q, j):
        mine = held[pair_rows(q, j), :].astype(bf)
        rows[pair_rows(q, j), :] = mine
        weight = enc_all[lax.div(q, 2), lax.rem(q, 2), :, weight_rows(j)]
        own_pairs(part, q, j)[...] = join_pair(dot(mine, weight, 1, 0)).astype(bf)

    def activate(h, acc):
        for k in range(pairs // CHAINS):
            j = h * (pairs // CHAINS) + k
            shift = bias_all[lax.div(me, 2), j // 2, pl.ds(2 * lax.rem(me, 2) + j % 2, 1), :]
            value, slope = gelu_parts(acc[k * per : (k + 1) * per] + shift)
            codes[y, x, j * per : (j + 1) * per] = value.astype(bf)
            slopes[j * per : (j + 1) * per, :] = slope

    stages = [v[k] for k in ("first", "second", "total")]
    reduce_share(
        ids, part, codes, *stages, v["ssend"].at[0], v["srecv"].at[0], groups(encode), activate,
        [lambda k=k: around.arrive(k) for k in range(1, 5)],
    )
    around.end()

    @pl.loop(0, HOMES)
    def _(q):
        for j in range(pairs):
            weight = dec_all[lax.div(q, 2), lax.rem(q, 2), weight_rows(j), :]
            held[pair_rows(q, j), :] = dot(split_pair(own_pairs(codes, q, j)[...]), weight, 1, 0)

    @pl.loop(0, HOMES, unroll=2)
    def _(home):
        hots = jnp.concatenate([slot_onehot(pos_all, home, slot, blocks, tok) for slot in range(CAP)], axis=0)
        at = [pl.ds(slot * HOMES + home, blocks, per) for slot in range(CAP)]
        some = jnp.concatenate([held[a, :].astype(bf) for a in at], axis=0)
        rebuilt = dot(some, hots, 0, 0)
        err = (rebuilt - tok_all[home].astype(f32).T).astype(bf)
        picked = dot(hots, err, 1, 1)
        for slot in range(CAP):
            held[at[slot], :] = picked[slot * blocks : (slot + 1) * blocks]

    def code_grad(q, j):
        err = held[pair_rows(q, j), :].astype(bf)
        weight = dec_all[lax.div(q, 2), lax.rem(q, 2), weight_rows(j), :]
        own_pairs(part, q, j)[...] = join_pair(dot(err, weight, 1, 1)).astype(bf)

    def dec_grad(q, j):
        err = held[pair_rows(q, j), :].astype(bf)
        return dot(split_pair(own_pairs(codes, q, j)[...]), err, 0, 0)

    def enc_grad(q, j):
        return dot(rows[pair_rows(q, j), :], split_pair(own_pairs(pgrad, q, j)[...]), 0, 0)

    def collect(m, grad, name, chain):
        out, half_in, narrow, z_in, sums = (v[name + k] for k in ("out", "half", "narrow", "z_in", "sums"))

        def slot(ref, j, *lead):
            return ref.at[(*lead, slice(None), weight_rows(j))] if m else ref.at[(*lead, weight_rows(j))]


        def cut_rows(way):
            cut = z_in.shape[2] // 2
            return pl.ds(way * cut, cut)

        def ring_on(d, n):
            ways = (0, 1) if d == 4 else (0,) if 0 < d < 4 else (1,) if d else ()
            for way in ways:
                k = min(d, 8 - d)
                src, dst = narrow.at[n % SLOTS], z_in.at[way, k - 1]
                if k == 4:
                    src, dst = narrow.at[n % SLOTS, cut_rows(way)], z_in.at[way, 3, cut_rows(way)]
                sems = [v[e].at[m, way, k - 1] for e in ("grsend", "grrecv")]
                chain[way, k] = send(src, dst, *sems, {"z": step(ids, "z", 1 - 2 * way)})

        def pass_on(copy, d, t, n):
            copy.wait()
            if d and n >= SLOTS:
                freed = FAR[n - SLOTS]
                for way in range(2) if freed == 4 else [int(freed > 4)]:
                    chain.pop((way, min(freed, 8 - freed))).wait_send()
            way, k = (0, d) if d < 4 else (1, 8 - d)
            if d == 0:
                chain[0, 1].wait_recv()
                chain[1, 1].wait_recv()
            elif d != 4:
                chain[way, k + 1].wait_recv()
            for j in range(pairs):
                acc = grad(2 * t + c, j) + slot(half_in, j, t)[...]
                if d and d != 4:
                    came = slot(z_in, j, way, k)
                    if k == 3 and m == 0:
                        if (j >= pairs // 2) == (way == 1):
                            acc += came[...].astype(f32)
                    elif k == 3:
                        cut = acc.shape[0] // 2
                        lower, upper = acc[:cut], acc[cut:]
                        if way == 0:
                            lower += came[:cut].astype(f32)
                        else:
                            upper += came[cut:].astype(f32)
                        acc = jnp.concatenate([lower, upper], axis=0)
                    else:
                        acc += came[...].astype(f32)
                if d == 0:
                    acc += slot(z_in, j, 0, 0)[...].astype(f32) + slot(z_in, j, 1, 0)[...].astype(f32)
                if d == 0:
                    slot(sums, j)[...] = acc
                else:
                    slot(narrow, j, n % SLOTS)[...] = acc.astype(bf)
            ring_on(d, n)

        last = None
        for k, d in enumerate(FAR):
            t = step(ids, "z", d)
            for j in range(pairs):
                slot(out, j, k % 2)[...] = grad(2 * t + 1 - c, j)
            copy = send(out.at[k % 2], half_in.at[t], v["csend"].at[m, k], v["crecv"].at[m, k], other)
            if last is not None:
                pass_on(*last)
            last = (copy, d, t, k)
            yield
        pass_on(*last)
        yield

    dec_chain, enc_chain = {}, {}
    dec_steps = collect(0, dec_grad, "d_", dec_chain)

    def advance(n):
        return lambda: [next(dec_steps) for _ in range(n)]

    def multiply(h, acc):
        at = pl.ds(h * acc.shape[0], acc.shape[0])
        pgrad[y, x, at] = (acc * slopes[at, :]).astype(bf)

    reduce_share(
        ids, part, pgrad, *stages, v["ssend"].at[1], v["srecv"].at[1], groups(code_grad), multiply,
        [advance(3), advance(2), advance(2), advance(2)],
    )
    for _ in collect(1, enc_grad, "e_", enc_chain):
        pass

    homes = []
    for m, name, chain, dst in ((0, "d_", dec_chain, dec_out), (1, "e_", enc_chain, enc_out)):
        sums = v[name + "sums"]
        for copy in chain.values():
            copy.wait_send()
        at = pl.ds(pl.multiple_of(c * lat, lat), lat)
        lanes = pl.ds(pl.multiple_of(lax.rem(x, 2) * LANES, LANES), LANES)
        items = []
        for t in range(4):
            piece = pl.ds(t * lat, lat)
            if m == 0:
                src, to = sums.at[piece], dst.at[at, lanes]
            else:
                src, to = sums.at[:, piece], dst.at[lanes, at]
            items.append(((m, t), (m, c, lax.rem(x, 2)), src, to, t, lax.div(x, 2)))
        homes += swap_homes(ids, items, _At(v["hsend"]), _At(v["hrecv"]))
    for m, dst in ((0, dec_out), (1, enc_out)):
        for h in range(2):
            for i in range(2):
                at, lanes = pl.ds(h * lat, lat), pl.ds(i * LANES, LANES)
                landed(dst.at[at, lanes] if m == 0 else dst.at[lanes, at], v["hrecv"].at[m, h, i])
    sent_homes(swaps)
    sent_homes(homes)


class _At:
    def __init__(self, ref):
        self.ref = ref

    @property
    def at(self):
        return self

    def __getitem__(self, index):
        return self.ref.at[index]


def sems(*shape):
    return pltpu.SemaphoreType.DMA(shape)


def local(
    tokens,
    block_ids,
    enc_bias,
    enc_master,
    dec_master,
    enc_first,
    enc_second,
    dec_first,
    dec_second,
):
    nz, nx = lax.axis_size("z"), lax.axis_size("x")
    ny, nc = lax.axis_size("y"), lax.axis_size("c")
    tok, width = tokens.shape
    lat, part = dec_master.shape
    blocks = lat // BLOCK * nz * nx
    half = lat // nc
    bf, f32 = jnp.bfloat16, jnp.float32

    per_half = half // BLOCK
    local_b = block_ids % (nc * per_half)
    shard = block_ids // (nc * per_half)
    place = (
        ((shard // nx) * nc + local_b // per_half) * nx + shard % nx
    ) * per_half + local_b % per_half

    per = CAP * HOMES
    rows_own = blocks // 2 // HOMES * per
    own_w = nx * half
    grid4 = (ny, nx, rows_own, LANES)
    w_enc, w_dec = (LANES, own_w), (own_w, LANES)
    scratch = {
        "enc": pltpu.VMEM((part, lat), bf),
        "dec": pltpu.VMEM((lat, part), bf),
        "held": pltpu.VMEM((blocks * per, LANES), f32),
        "rows": pltpu.VMEM((blocks * per, LANES), bf),
        "part": pltpu.VMEM(grid4, bf),
        "codes": pltpu.VMEM(grid4, bf),
        "pgrad": pltpu.VMEM(grid4, bf),
        "tok_all": pltpu.VMEM((HOMES, tok, LANES), bf),
        "pos_all": pltpu.VMEM((HOMES, 8, tok), jnp.int32),
        "enc_all": pltpu.VMEM((nz, nc) + w_enc, bf),
        "dec_all": pltpu.VMEM((nz, nc) + w_dec, bf),
        "slopes": pltpu.VMEM((rows_own, LANES), f32),
        "bias_all": pltpu.VMEM((nz, nx, lat // LANES, LANES), f32),
        "first": pltpu.VMEM((CHAINS, 3, 4, rows_own // CHAINS, LANES), bf),
        "second": pltpu.VMEM((CHAINS, 3, rows_own // CHAINS, LANES), f32),
        "total": pltpu.VMEM((CHAINS, 4, rows_own // CHAINS, LANES), f32),
    }
    for name, shape in (("d_", w_dec), ("e_", w_enc)):
        scratch[name + "out"] = pltpu.VMEM((2,) + shape, f32)
        scratch[name + "half"] = pltpu.VMEM((nz,) + shape, f32)
        scratch[name + "narrow"] = pltpu.VMEM((SLOTS,) + shape, bf)
        scratch[name + "z_in"] = pltpu.VMEM((2, nz // 2) + shape, bf)
        scratch[name + "sums"] = pltpu.VMEM(shape, f32)
    for name, shape in (
        ("w", (2, 2, 2)), ("b", (3,)), ("t", (15,)), ("p", (15,)), ("er", (2, 4, 2)), ("ec", (8,)),
        ("dr", (2, 4, 2)), ("dc", (8,)), ("bz", (7,)), ("s", (2, 4, CHAINS, 3)), ("gr", (2, 2, 4)), ("c", (2, 8)),
    ):
        scratch[name + "send"] = sems(*shape)
        scratch[name + "recv"] = sems(*((2, 4) if name == "w" else shape))
    scratch.update(lsem=sems(2), hsend=sems(2, 4), hrecv=sems(2, 2, 2))

    vmem = pl.BlockSpec(memory_space=pltpu.VMEM)
    enc_share, dec_share = pl.pallas_call(
        functools.partial(train_kernel, tuple(scratch)),
        out_shape=[jax.ShapeDtypeStruct((part, lat), f32), jax.ShapeDtypeStruct((lat, part), f32)],
        in_specs=[pl.BlockSpec(memory_space=pl.ANY)] + [vmem] * 4,
        out_specs=[vmem] * 2,
        scratch_shapes=list(scratch.values()),
        compiler_params=pltpu.CompilerParams(
            collective_id=1, has_side_effects=True, vmem_limit_bytes=VMEM
        ),
        name="train",
    )(tokens, place.T, enc_master, dec_master, enc_bias.reshape(-1, LANES))
    enc_new, enc_first_new, enc_second_new = adam(enc_master, enc_share, enc_first, enc_second)
    dec_new, dec_first_new, dec_second_new = adam(dec_master, dec_share, dec_first, dec_second)
    return (enc_new, dec_new, enc_first_new, enc_second_new, dec_first_new, dec_second_new)


def solution(mesh):
    grid = Mesh(mesh.devices.reshape(8, 4, 4, 2), ("z", "x", "y", "c"))
    lat, rep = ("z", "x"), REP
    tok = P(rep + lat, None)
    enc, dec = P(rep, lat), P(lat, rep)
    return jax.shard_map(
        local,
        mesh=grid,
        in_specs=(tok, tok, P(lat), enc, dec, enc, enc, dec, dec),
        out_specs=(enc, dec, enc, enc, dec, dec),
        check_vma=False,
    )
```
